128 devices in a mesh: seq: 16 (over x, y_hi, core), res: 8 (over z, y_lo).
Axes of the slice: x: 4, y: 4 (y_hi: 2, y_lo: 2; y = y_hi * 2 + y_lo), z: 4, core: 2. Of those that a mesh axis runs over, the one named last changes fastest.
Arguments:
- left_alignment: bfloat16 [256, 256, 32], P('seq', 'res'), may hold values from -6 to 6
- right_alignment: bfloat16 [256, 256, 32], P('seq', 'res'), may hold values from -6 to 6
- alignment_mask: int32 [256, 256], P('seq', 'res'), may hold values from 0 to 1, as said below
- output_weight: bfloat16 [32, 32, 128], replicated, may hold values from -3 to 3
- output_bias: float32 [128], replicated, may hold values from -4 to 4
- pair_update_cotangent: bfloat16 [256, 256, 128], P('seq', 'res'), may hold values from -6 to 6
Outputs:
- pair_update: bfloat16 [256, 256, 128], P('seq', 'res')
- left_operand_gradient: float32 [256, 256, 32], P('seq', 'res')
- right_operand_gradient: float32 [256, 256, 32], P('seq', 'res')
- weight_grad: float32 [32, 32, 128], replicated
- bias_grad: float32 [128], replicated
The draws below stay inside these ranges and needn't reach their ends.
Inputs may be any that keep to these rules, and one draw needn't show every extreme that they name: alignment_mask is 0 or 1; sequence 0 is 1 at every residue.
All inputs are finite; a program needn't handle non-finite values.
Results may differ from the reference program's by a relative error of at most 0.0049.
Values may be sent and summed in bfloat16 or wider, within the bound.
No kernel may reach another device: no remote copies, remote signals or barrier semaphores. Data moves between devices by JAX's collectives and lax.ppermute only.
A program may use at most 256 MiB of HBM per device.

```python
import jax
import jax.numpy as jnp
from jax import lax

OPERAND_CHANNELS = 32
PAIR_CH = 128
ALIGNMENT_COUNT = 256
CROP_RESIDUES = 256


def draw_alignment_mask(key, part):
    key = jax.random.fold_in(key, 11)
    rotation_random_key, shift_random_key = jax.random.split(key)
    sequence_index = jnp.arange(ALIGNMENT_COUNT, dtype=jnp.int32)[:, None]
    tree_level = 90 - 60 * sequence_index // ALIGNMENT_COUNT + jax.random.randint(shift_random_key, (1, CROP_RESIDUES), -10, 11, dtype=jnp.int32)
    rotated_values = jax.random.randint(rotation_random_key, (ALIGNMENT_COUNT, CROP_RESIDUES), 0, 100, dtype=jnp.int32)
    covered = (rotated_values < tree_level).astype(jnp.int32)
    return jnp.where(sequence_index == 0, 1, covered).astype(jnp.int32)


def block_scale(key, shape, shards, least, largest):
    factor_of = 1.0
    for dim, blocks in shards:
        steps = jax.random.uniform(jax.random.fold_in(jax.random.fold_in(key, 6), dim), (blocks,), jnp.float32, least / len(shards), largest / len(shards))
        factor_of = factor_of * jnp.repeat(jnp.exp(steps), shape[dim] // blocks).reshape((-1,) + (1,) * (len(shape) - 1 - dim))
    return factor_of


def normal_values(key, extent, deviation, limit, cuts=(), kind=jnp.bfloat16):
    values = jax.random.normal(key, extent, jnp.float32) * deviation
    if len(cuts) > 0:
        values = block_scale(key, extent, cuts, -0.22, 0.18) * values
    return jnp.clip(values, min=-limit, max=limit).astype(kind)


def setup_inputs(seed: int = 0) -> dict:
    seeds = jax.random.split(jax.random.key(seed), 7)
    return {
        "left_alignment": normal_values(seeds[0], (ALIGNMENT_COUNT, CROP_RESIDUES, OPERAND_CHANNELS), 1.0, 6.0, ((0, 16), (1, 8))),
        "right_alignment": normal_values(seeds[1], (ALIGNMENT_COUNT, CROP_RESIDUES, OPERAND_CHANNELS), 1.0, 6.0, ((0, 16), (1, 8))),
        "alignment_mask": draw_alignment_mask(jax.random.fold_in(seeds[6], 71), 0),
        "output_weight": normal_values(seeds[3], (OPERAND_CHANNELS, OPERAND_CHANNELS, PAIR_CH), 4 ** -0.5, 3.0),
        "output_bias": normal_values(seeds[4], (PAIR_CH,), 1.0, 4.0, (), jnp.float32),
        "pair_update_cotangent": normal_values(seeds[5], (CROP_RESIDUES, CROP_RESIDUES, PAIR_CH), 1.0, 6.0, ((0, 16), (1, 8))),
    }


def reference(left_alignment, right_alignment, alignment_mask, output_weight, output_bias, pair_update_cotangent):
    block_list = ALIGNMENT_COUNT // 8
    mask_float = alignment_mask.astype(jnp.float32)
    mask_bfloat = alignment_mask.astype(jnp.bfloat16)
    left_under_mask = left_alignment * mask_bfloat[:, :, None]
    right_under_mask = right_alignment * mask_bfloat[:, :, None]
    weight32 = output_weight.astype(jnp.float32)
    counts = jnp.dot(mask_float.T, mask_float, precision=lax.Precision.HIGHEST) + 1e-3
    left_blocks = left_under_mask.reshape(block_list, 8, CROP_RESIDUES, OPERAND_CHANNELS)
    right_blocks = right_under_mask.reshape(block_list, 8, CROP_RESIDUES, OPERAND_CHANNELS)
    mask_blocks = mask_float.reshape(block_list, 8, CROP_RESIDUES)

    def project(right_part):
        proj = jnp.einsum("sjd,cdh->scjh", right_part.astype(jnp.float32), weight32)
        return proj.astype(jnp.bfloat16).reshape(8 * OPERAND_CHANNELS, CROP_RESIDUES * PAIR_CH)

    def left_rows(left_part):
        return left_part.transpose(1, 0, 2).reshape(CROP_RESIDUES, 8 * OPERAND_CHANNELS)

    def forward_step(summed, parts):
        left_part, right_part = parts
        summed = summed + jnp.dot(left_rows(left_part), project(right_part), preferred_element_type=jnp.float32)
        return summed, None

    summed, unused = lax.scan(forward_step, jnp.zeros((CROP_RESIDUES, CROP_RESIDUES * PAIR_CH), jnp.float32), (left_blocks, right_blocks))
    summed = summed.reshape(CROP_RESIDUES, CROP_RESIDUES, PAIR_CH)
    pair_update = (summed / counts[:, :, None] + output_bias).astype(jnp.bfloat16)
    scaled = (pair_update_cotangent.astype(jnp.float32) / counts[:, :, None]).astype(jnp.bfloat16)
    scaled_flat = scaled.reshape(CROP_RESIDUES, CROP_RESIDUES * PAIR_CH)

    def backward_step(wacc, parts):
        left_part, right_part, mask_part = parts
        proj = project(right_part)
        rows = left_rows(left_part)
        proj_grad = jnp.dot(rows.T, scaled_flat, preferred_element_type=jnp.float32)
        left_part_grad = jnp.dot(scaled_flat, proj.T, preferred_element_type=jnp.float32)
        left_part_grad = left_part_grad.reshape(CROP_RESIDUES, 8, OPERAND_CHANNELS).transpose(1, 0, 2) * mask_part[:, :, None]
        grad4 = proj_grad.reshape(8, OPERAND_CHANNELS, CROP_RESIDUES, PAIR_CH)
        right_part_grad = jnp.einsum("scjh,cdh->sjd", grad4, weight32, precision=lax.Precision.HIGHEST) * mask_part[:, :, None]
        wacc = wacc + jnp.einsum("sjd,scjh->cdh", right_part.astype(jnp.float32), grad4, precision=lax.Precision.HIGHEST)
        return wacc, (left_part_grad, right_part_grad)

    weight_grad, gradient_tuple = lax.scan(backward_step, jnp.zeros((OPERAND_CHANNELS, OPERAND_CHANNELS, PAIR_CH), jnp.float32), (left_blocks, right_blocks, mask_blocks))
    left_operand_gradient = gradient_tuple[0].reshape(ALIGNMENT_COUNT, CROP_RESIDUES, OPERAND_CHANNELS)
    right_operand_gradient = gradient_tuple[1].reshape(ALIGNMENT_COUNT, CROP_RESIDUES, OPERAND_CHANNELS)
    bias_grad = jnp.sum(pair_update_cotangent.astype(jnp.float32), axis=(0, 1))
    return pair_update, left_operand_gradient, right_operand_gradient, weight_grad, bias_grad
```

```python
import jax
import jax.numpy as jnp
from jax import lax
from jax.experimental import pallas as pl
from jax.experimental.pallas import tpu as pltpu
from jax.sharding import PartitionSpec as P

F32 = jnp.float32
BF16 = jnp.bfloat16
ROWS_ROWS = (((0,), (0,)), ((), ()))
LANES_LANES = (((1,), (1,)), ((), ()))


def iota(shape, dim):
    return lax.broadcasted_iota(jnp.int32, shape, dim)


def swap_groups(blocks):
    lane = iota(blocks[0].shape, 1)
    upper = lane >= 64
    odd = (lane // 32) % 2 == 1
    b0, b1, b2, b3 = blocks
    r0, r1, r2, r3 = (pltpu.roll(b, 64, 1) for b in blocks)
    b0, b2 = jnp.where(upper, r2, b0), jnp.where(upper, b2, r0)
    b1, b3 = jnp.where(upper, r3, b1), jnp.where(upper, b3, r1)
    up1, up3 = pltpu.roll(b1, 32, 1), pltpu.roll(b3, 32, 1)
    down0, down2 = pltpu.roll(b0, 96, 1), pltpu.roll(b2, 96, 1)
    return (
        jnp.where(odd, up1, b0),
        jnp.where(odd, b1, down0),
        jnp.where(odd, up3, b2),
        jnp.where(odd, b3, down2),
    )


def pair_kernel(
    g_ref, w_ref, bias_ref, cot_ref, pair_ref, msg_ref, bsum_ref,
    y_ref, x_ref, dx_ref, dy_ref, plain_ref, cot32_ref, scaled_ref,
):
    row, col = iota((256, 256), 0), iota((256, 256), 1)
    order = (col == (row % 16) * 16 + row // 16).astype(F32).astype(BF16)
    g = jnp.dot(order, g_ref[...], preferred_element_type=F32).astype(BF16)
    masks = g[:, 1536:]
    spread_i = (iota((128, 512), 0) == iota((128, 512), 1) % 16).astype(F32).astype(BF16)
    spread_jd = (iota((128, 1024), 0) == 16 + iota((128, 1024), 1) // 32).astype(F32).astype(BF16)
    lane = iota((128, 512), 1)
    spread_j = (iota((128, 512), 0) == 16 + 4 * ((lane // 16) % 8) + lane // 128).astype(F32).astype(BF16)
    mask_i = jnp.dot(masks, spread_i, preferred_element_type=F32)
    mask_jd = jnp.dot(masks, spread_jd, preferred_element_type=F32)
    mask_j = jnp.dot(masks, spread_j, preferred_element_type=F32)
    left = g[:, :512] * mask_i.astype(BF16)
    right = g[:, 512:1536] * mask_jd.astype(BF16)
    both = (mask_i * mask_j).astype(BF16)
    counts = (
        lax.dot_general(both, jnp.ones((256, 128), BF16), ROWS_ROWS, preferred_element_type=F32) + 1e-3
    )

    cot32 = cot_ref[...].astype(F32)
    cot32_ref[...] = cot32
    bsum_ref[...] = jnp.sum(cot32, axis=0, keepdims=True)
    for j in range(32):
        at = ((j % 4) * 8 + j // 4) * 16
        scaled_ref[at : at + 16, :] = (
            cot32_ref[pl.ds(j, 16, stride=32), :] / counts[at : at + 16, :]
        ).astype(BF16)

    y_ref[...] = lax.dot_general(left, right, ROWS_ROWS, preferred_element_type=F32)
    for u in range(8):
        lanes = slice(u * 128, u * 128 + 128)
        for t in range(8):
            tiles = swap_groups([y_ref[f * 128 + t * 16 : f * 128 + t * 16 + 16, lanes] for f in range(4)])
            for e in range(4):
                at = (e * 8 + u) * 16
                x_ref[at : at + 16, t * 128 : t * 128 + 128] = tiles[e].astype(BF16)

    summed = jnp.dot(x_ref[...], w_ref[...], preferred_element_type=F32)
    update = summed / counts + bias_ref[...]
    for j in range(32):
        at = ((j % 4) * 8 + j // 4) * 16
        plain_ref[pl.ds(j, 16, stride=32), :] = update[at : at + 16, :]
    pair_ref[...] = plain_ref[...].astype(BF16)

    scaled = scaled_ref[...]
    dx_ref[...] = lax.dot_general(scaled, w_ref[...], LANES_LANES, preferred_element_type=F32)
    for u in range(8):
        lanes = slice(u * 128, u * 128 + 128)
        for t in range(8):
            tiles = swap_groups(
                [dx_ref[(e * 8 + u) * 16 : (e * 8 + u) * 16 + 16, t * 128 : t * 128 + 128] for e in range(4)]
            )
            for f in range(4):
                dy_ref[f * 128 + t * 16 : f * 128 + t * 16 + 16, lanes] = tiles[f].astype(BF16)

    weight_part = lax.dot_general(x_ref[...], scaled, ROWS_ROWS, preferred_element_type=F32)
    right_part = jnp.dot(left, dy_ref[...], preferred_element_type=F32) * mask_jd
    left_part = lax.dot_general(right, dy_ref[...], LANES_LANES, preferred_element_type=F32) * mask_i
    for m in range(128):
        s, k = m // 8, m % 8
        msg_ref[m, 0:16, :] = right_part[s * 16 : s * 16 + 16, k * 128 : k * 128 + 128].astype(BF16)
        at = s * 16 + (k % 2) * 8
        msg_ref[m, 16:32, :] = jnp.concatenate(
            [weight_part[m * 8 : m * 8 + 8, :], left_part[at : at + 8, (k // 2) * 128 : (k // 2) * 128 + 128]], 0
        ).astype(BF16)


def reduce_kernel(in_ref, bsum_ref, out_ref, rows_ref):
    half = lax.rem(lax.axis_index("res"), 2)
    weight = jnp.zeros((8, 128), F32)
    for r in range(8):
        total = jnp.zeros((16, 128), F32)
        for q in range(16):
            total = total + in_ref[q * 8 + r, 0:16, :].astype(F32)
        rows_ref[pl.ds(r * 8, 16, stride=64), :] = total
    for q in range(16):
        total = jnp.zeros((16, 128), F32)
        for r in range(8):
            total = total + in_ref[q * 8 + r, 16:32, :].astype(F32)
        weight = weight + total[0:8]
        for side in range(2):
            at = side * 512 + (q // 2) * 8 + 1 + q % 2
            rows_ref[pl.ds(at, 8, stride=64), :] = jnp.where(half == side, total[8:16], 0.0)
    bias = jnp.broadcast_to(bsum_ref[...], (8, 128))
    high = bias.astype(BF16).astype(F32)
    low = bias - high
    sub = iota((8, 128), 0)
    for m in range(128):
        rows = rows_ref[m * 8 : m * 8 + 8, :]
        rows = jnp.where(sub < 3, rows, jnp.where(sub == 3, high, jnp.where(sub == 4, low, 0.0)))
        out_ref[m] = jnp.concatenate([weight, rows], 0).astype(BF16)


def final_kernel(in_ref, weight_ref, right_ref, left_ref, bias_ref, rows_ref):
    total = jnp.zeros((8, 128), F32)
    for m in range(128):
        block = in_ref[m].astype(F32)
        weight_ref[m * 8 : m * 8 + 8, :] = block[0:8]
        rows_ref[m * 8 : m * 8 + 8, :] = block[8:16]
        total = total + block[8:16]
    right_ref[...] = rows_ref[pl.ds(0, 128, stride=8), :]
    for h in range(2):
        left_ref[h] = rows_ref[pl.ds(1 + h, 64, stride=16), :] + rows_ref[pl.ds(9 + h, 64, stride=16), :]
    bias_ref[...] = total[3:4] + total[4:5]


def call(kernel, outs, scratch, *args):
    whole = pl.BlockSpec(memory_space=pltpu.VMEM)
    return pl.pallas_call(
        kernel,
        out_shape=outs,
        in_specs=[whole] * len(args),
        out_specs=tuple([whole] * len(outs)),
        scratch_shapes=scratch,
        compiler_params=pltpu.CompilerParams(vmem_limit_bytes=40 * 1024 * 1024),
    )(*args)


def shape(dims, dtype):
    return jax.ShapeDtypeStruct(dims, dtype)


def per_device(left, right, mask, weight, bias, cotangent):
    mask = mask.astype(BF16)
    left = left.reshape(16, 2, 16, 8, 4).transpose(1, 0, 4, 3, 2).reshape(2, 16, 512)
    mask_i = jnp.pad(mask.reshape(16, 2, 16).transpose(1, 0, 2), ((0, 0), (0, 0), (0, 112)))
    block = jnp.concatenate([left, mask_i], -1)
    block = lax.all_to_all(jnp.broadcast_to(block, (8, 2, 16, 640)), "res", 0, 0, tiled=True)
    block = block.reshape(16, 16, 640)
    mask_j = jnp.pad(mask, ((0, 0), (16, 80)))
    block = jnp.concatenate(
        [
            block[:, :, :512],
            jnp.broadcast_to(right.reshape(16, 1024), (16, 16, 1024)),
            block[:, :, 512:] + mask_j,
        ],
        -1,
    )
    block = lax.all_to_all(block, "seq", 0, 0, tiled=True).reshape(256, 1664)

    pair_update, parts, bias_part = call(
        pair_kernel,
        (shape((512, 128), BF16), shape((128, 32, 128), BF16), shape((1, 128), F32)),
        [
            pltpu.VMEM((512, 1024), F32),
            pltpu.VMEM((512, 1024), BF16),
            pltpu.VMEM((512, 1024), F32),
            pltpu.VMEM((512, 1024), BF16),
            pltpu.VMEM((512, 128), F32),
            pltpu.VMEM((512, 128), F32),
            pltpu.VMEM((512, 128), BF16),
        ],
        block,
        weight.reshape(1024, 128),
        bias.reshape(1, 128),
        cotangent.reshape(512, 128),
    )
    parts = lax.all_to_all(parts, ("seq", "res"), 0, 0, tiled=True)
    (sums,) = call(
        reduce_kernel, (shape((128, 16, 128), BF16),), [pltpu.VMEM((1024, 128), F32)], parts, bias_part
    )
    sums = lax.all_to_all(sums, ("seq", "res"), 0, 0, tiled=True)
    weight_grad, right_grad, left_grad, bias_grad = call(
        final_kernel,
        (shape((1024, 128), F32), shape((128, 128), F32), shape((2, 64, 128), F32), shape((1, 128), F32)),
        [pltpu.VMEM((1024, 128), F32)],
        sums,
    )
    left_grad = left_grad.reshape(2, 16, 4, 8, 16).transpose(1, 0, 4, 3, 2).reshape(16, 32, 32)
    return (
        pair_update.reshape(16, 32, 128),
        left_grad,
        right_grad.reshape(16, 32, 32),
        weight_grad.reshape(32, 32, 128),
        bias_grad.reshape(128),
    )


def solution(mesh):
    return jax.shard_map(
        per_device,
        mesh=mesh,
        in_specs=(
            P("seq", "res", None),
            P("seq", "res", None),
            P("seq", "res"),
            P(),
            P(),
            P("seq", "res", None),
        ),
        out_specs=(P("seq", "res", None), P("seq", "res", None), P("seq", "res", None), P(), P()),
        check_vma=False,
    )
```

```python
import jax
import jax.numpy as jnp
from jax import lax
from jax.experimental import pallas as pl
from jax.experimental.pallas import tpu as pltpu
from jax.sharding import PartitionSpec as P

F32 = jnp.float32
BF16 = jnp.bfloat16
ROWS_ROWS = (((0,), (0,)), ((), ()))
LANES_LANES = (((1,), (1,)), ((), ()))


def iota(shape, dim):
    return lax.broadcasted_iota(jnp.int32, shape, dim)


def swap_groups(blocks):
    lane = iota(blocks[0].shape, 1)
    upper = lane >= 64
    odd = (lane // 32) % 2 == 1
    b0, b1, b2, b3 = blocks
    r0, r1, r2, r3 = (pltpu.roll(b, 64, 1) for b in blocks)
    b0, b2 = jnp.where(upper, r2, b0), jnp.where(upper, b2, r0)
    b1, b3 = jnp.where(upper, r3, b1), jnp.where(upper, b3, r1)
    up1, up3 = pltpu.roll(b1, 32, 1), pltpu.roll(b3, 32, 1)
    down0, down2 = pltpu.roll(b0, 96, 1), pltpu.roll(b2, 96, 1)
    return (
        jnp.where(odd, up1, b0),
        jnp.where(odd, b1, down0),
        jnp.where(odd, up3, b2),
        jnp.where(odd, b3, down2),
    )


def choose(condition):
    return condition.astype(F32).astype(BF16)


def channel_lanes():
    lane = iota((32, 512), 1)
    return choose(iota((32, 512), 0) == 4 * ((lane % 128) // 16) + lane // 128)


def own_residue():
    return iota((512, 512), 0) % 16 == iota((512, 512), 1) % 16


def prep_kernel(left_hbm, mask_hbm, out_ref, left_ref, mask_ref, sems):
    copies = [
        pltpu.make_async_copy(left_hbm, left_ref, sems.at[0]),
        pltpu.make_async_copy(mask_hbm, mask_ref, sems.at[1]),
    ]
    for copy in copies:
        copy.start()
    for copy in copies:
        copy.wait()
    spread = jnp.dot(left_ref[...], channel_lanes(), preferred_element_type=F32)
    spread = jnp.where(own_residue(), spread, 0.0).astype(BF16)
    row, col = iota((32, 512), 0), iota((32, 512), 1)
    gather = choose((col // 32 == row % 16) & ((col % 32) // 16 == row // 16))
    block = jnp.dot(gather, spread, preferred_element_type=F32).astype(BF16)
    mask = mask_ref[...].astype(F32).astype(BF16)
    row, col = iota((32, 128), 0), iota((32, 128), 1)
    halves = [
        jnp.dot(mask, choose((row == h * 16 + col) & (col < 16)), preferred_element_type=F32)
        for h in range(2)
    ]
    masks = jnp.concatenate(halves, 0).astype(BF16)
    for r in range(8):
        out_ref[r, :, 0:512] = block
        out_ref[r, :, 512:640] = masks


def pair_kernel(
    g_ref, w_ref, bias_ref, cot_ref, pair_ref, msg_ref, bsum_ref,
    y_ref, x_ref, dx_ref, dy_ref, plain_ref, cot32_ref, scaled_ref,
):
    row, col = iota((256, 256), 0), iota((256, 256), 1)
    order = (col == (row % 16) * 16 + row // 16).astype(F32).astype(BF16)
    g = jnp.dot(order, g_ref[...], preferred_element_type=F32).astype(BF16)
    masks = g[:, 1536:]
    spread_i = (iota((128, 512), 0) == iota((128, 512), 1) % 16).astype(F32).astype(BF16)
    spread_jd = (iota((128, 1024), 0) == 16 + iota((128, 1024), 1) // 32).astype(F32).astype(BF16)
    lane = iota((128, 512), 1)
    spread_j = (iota((128, 512), 0) == 16 + 4 * ((lane // 16) % 8) + lane // 128).astype(F32).astype(BF16)
    mask_i = jnp.dot(masks, spread_i, preferred_element_type=F32)
    mask_jd = jnp.dot(masks, spread_jd, preferred_element_type=F32)
    mask_j = jnp.dot(masks, spread_j, preferred_element_type=F32)
    left = g[:, :512] * mask_i.astype(BF16)
    right = g[:, 512:1536] * mask_jd.astype(BF16)
    both = (mask_i * mask_j).astype(BF16)
    counts = (
        lax.dot_general(both, jnp.ones((256, 128), BF16), ROWS_ROWS, preferred_element_type=F32) + 1e-3
    )

    inverse = 1.0 / counts
    cot32 = cot_ref[...].astype(F32)
    cot32_ref[...] = cot32
    bsum_ref[...] = jnp.sum(cot32, axis=0, keepdims=True)
    for j in range(32):
        at = ((j % 4) * 8 + j // 4) * 16
        scaled_ref[at : at + 16, :] = (
            cot32_ref[pl.ds(j, 16, stride=32), :] * inverse[at : at + 16, :]
        ).astype(BF16)
    scaled = scaled_ref[...]

    y_ref[...] = lax.dot_general(left, right, ROWS_ROWS, preferred_element_type=F32)
    for u in range(8):
        lanes = slice(u * 128, u * 128 + 128)
        for t in range(8):
            tiles = swap_groups([y_ref[f * 128 + t * 16 : f * 128 + t * 16 + 16, lanes] for f in range(4)])
            for e in range(4):
                at = (e * 8 + u) * 16
                x_ref[at : at + 16, t * 128 : t * 128 + 128] = tiles[e].astype(BF16)

    dx_ref[...] = lax.dot_general(scaled, w_ref[...], LANES_LANES, preferred_element_type=F32)
    for u in range(8):
        lanes = slice(u * 128, u * 128 + 128)
        for t in range(8):
            tiles = swap_groups(
                [dx_ref[(e * 8 + u) * 16 : (e * 8 + u) * 16 + 16, t * 128 : t * 128 + 128] for e in range(4)]
            )
            for f in range(4):
                dy_ref[f * 128 + t * 16 : f * 128 + t * 16 + 16, lanes] = tiles[f].astype(BF16)

    update = jnp.dot(x_ref[...], w_ref[...], preferred_element_type=F32) * inverse + bias_ref[...]
    for j in range(32):
        at = ((j % 4) * 8 + j // 4) * 16
        plain_ref[pl.ds(j, 16, stride=32), :] = update[at : at + 16, :]
    pair_ref[...] = plain_ref[...].astype(BF16)

    weight_part = lax.dot_general(x_ref[...], scaled, ROWS_ROWS, preferred_element_type=F32)
    right_part = jnp.dot(left, dy_ref[...], preferred_element_type=F32) * mask_jd
    left_part = lax.dot_general(right, dy_ref[...], LANES_LANES, preferred_element_type=F32) * mask_i
    for m in range(128):
        s, k = m // 8, m % 8
        msg_ref[m, 0:16, :] = right_part[s * 16 : s * 16 + 16, k * 128 : k * 128 + 128].astype(BF16)
        at = s * 16 + (k % 2) * 8
        msg_ref[m, 16:32, :] = jnp.concatenate(
            [weight_part[m * 8 : m * 8 + 8, :], left_part[at : at + 8, (k // 2) * 128 : (k // 2) * 128 + 128]], 0
        ).astype(BF16)


def reduce_kernel(in_ref, bsum_ref, out_ref, rows_ref):
    half = lax.rem(lax.axis_index("res"), 2)
    weight = jnp.zeros((8, 128), F32)
    for r in range(8):
        total = jnp.zeros((16, 128), F32)
        for q in range(16):
            total = total + in_ref[q * 8 + r, 0:16, :].astype(F32)
        rows_ref[pl.ds(r * 8, 16, stride=64), :] = total
    for q in range(16):
        total = jnp.zeros((16, 128), F32)
        for r in range(8):
            total = total + in_ref[q * 8 + r, 16:32, :].astype(F32)
        weight = weight + total[0:8]
        for side in range(2):
            at = side * 512 + (q // 2) * 8 + 1 + q % 2
            rows_ref[pl.ds(at, 8, stride=64), :] = jnp.where(half == side, total[8:16], 0.0)
    bias = jnp.broadcast_to(bsum_ref[...], (8, 128))
    high = bias.astype(BF16).astype(F32)
    low = bias - high
    sub = iota((8, 128), 0)
    for m in range(128):
        rows = rows_ref[m * 8 : m * 8 + 8, :]
        rows = jnp.where(sub < 3, rows, jnp.where(sub == 3, high, jnp.where(sub == 4, low, 0.0)))
        out_ref[m] = jnp.concatenate([weight, rows], 0).astype(BF16)


def final_kernel(in_ref, weight_ref, right_ref, left_ref, bias_ref, rows_ref):
    total = jnp.zeros((8, 128), F32)
    for m in range(128):
        block = in_ref[m].astype(F32)
        weight_ref[m * 8 : m * 8 + 8, :] = block[0:8]
        rows_ref[m * 8 : m * 8 + 8, :] = block[8:16]
        total = total + block[8:16]
    for k in range(8):
        tile = rows_ref[pl.ds(k * 8, 16, stride=64), :]
        for e in range(4):
            right_ref[pl.ds(k * 4 + e, 16, stride=32), :] = tile[:, e * 32 : e * 32 + 32]
    left = jnp.concatenate(
        [
            jnp.concatenate(
                [
                    rows_ref[pl.ds(f * 16 + 1 + h, 16, stride=64), :]
                    + rows_ref[pl.ds(f * 16 + 9 + h, 16, stride=64), :]
                    for f in range(4)
                ],
                1,
            )
            for h in range(2)
        ],
        0,
    ).astype(BF16)
    row, col = iota((512, 32), 0), iota((512, 32), 1)
    scatter = choose((row // 32 == col % 16) & ((row % 32) // 16 == col // 16))
    spread = jnp.dot(scatter, left, preferred_element_type=F32)
    spread = jnp.where(own_residue(), spread, 0.0).astype(BF16)
    left_ref[...] = lax.dot_general(spread, channel_lanes(), LANES_LANES, preferred_element_type=F32)
    bias_ref[...] = total[3:4] + total[4:5]


def call(kernel, outs, scratch, *args, space=pltpu.VMEM, mib=40):
    whole = pl.BlockSpec(memory_space=pltpu.VMEM)
    return pl.pallas_call(
        kernel,
        out_shape=outs,
        in_specs=[pl.BlockSpec(memory_space=space)] * len(args),
        out_specs=tuple([whole] * len(outs)),
        scratch_shapes=scratch,
        compiler_params=pltpu.CompilerParams(vmem_limit_bytes=mib * 1024 * 1024),
    )(*args)


def shape(dims, dtype):
    return jax.ShapeDtypeStruct(dims, dtype)


def per_device(left, right, mask, weight, bias, cotangent):
    (block,) = call(
        prep_kernel,
        (shape((8, 32, 640), BF16),),
        [pltpu.VMEM((512, 32), BF16), pltpu.VMEM((16, 32), jnp.int32), pltpu.SemaphoreType.DMA((2,))],
        left.reshape(512, 32),
        mask,
        space=pltpu.HBM,
        mib=60,
    )
    block = lax.all_to_all(block, "res", 0, 0, tiled=True)
    block, right, mask = lax.optimization_barrier((block, right, mask))
    block = block.reshape(16, 16, 640)
    mask_j = jnp.pad(mask.astype(BF16), ((0, 0), (16, 80)))
    block = jnp.concatenate(
        [
            block[:, :, :512],
            jnp.broadcast_to(right.reshape(16, 1024), (16, 16, 1024)),
            block[:, :, 512:] + mask_j,
        ],
        -1,
    )
    block = lax.all_to_all(block, "seq", 0, 0, tiled=True).reshape(256, 1664)

    pair_update, parts, bias_part = call(
        pair_kernel,
        (shape((512, 128), BF16), shape((128, 32, 128), BF16), shape((1, 128), F32)),
        [
            pltpu.VMEM((512, 1024), F32),
            pltpu.VMEM((512, 1024), BF16),
            pltpu.VMEM((512, 1024), F32),
            pltpu.VMEM((512, 1024), BF16),
            pltpu.VMEM((512, 128), F32),
            pltpu.VMEM((512, 128), F32),
            pltpu.VMEM((512, 128), BF16),
        ],
        block,
        weight.reshape(1024, 128),
        bias.reshape(1, 128),
        cotangent.reshape(512, 128),
    )
    parts = lax.all_to_all(parts, ("seq", "res"), 0, 0, tiled=True)
    (sums,) = call(
        reduce_kernel, (shape((128, 16, 128), BF16),), [pltpu.VMEM((1024, 128), F32)], parts, bias_part
    )
    sums = lax.all_to_all(sums, ("seq", "res"), 0, 0, tiled=True)
    weight_grad, right_grad, left_grad, bias_grad = call(
        final_kernel,
        (shape((1024, 128), F32), shape((512, 32), F32), shape((512, 32), F32), shape((1, 128), F32)),
        [pltpu.VMEM((1024, 128), F32)],
        sums,
    )
    return (
        pair_update.reshape(16, 32, 128),
        left_grad.reshape(16, 32, 32),
        right_grad.reshape(16, 32, 32),
        weight_grad.reshape(32, 32, 128),
        bias_grad.reshape(128),
    )


def solution(mesh):
    return jax.shard_map(
        per_device,
        mesh=mesh,
        in_specs=(
            P("seq", "res", None),
            P("seq", "res", None),
            P("seq", "res"),
            P(),
            P(),
            P("seq", "res", None),
        ),
        out_specs=(P("seq", "res", None), P("seq", "res", None), P("seq", "res", None), P(), P()),
        check_vma=False,
    )
```

```python
import jax
import jax.numpy as jnp
from jax import lax
from jax.experimental import pallas as pl
from jax.experimental.pallas import tpu as pltpu
from jax.sharding import Mesh
from jax.sharding import PartitionSpec as P

F32 = jnp.float32
BF16 = jnp.bfloat16
ROWS_ROWS = (((0,), (0,)), ((), ()))
LANES_LANES = (((1,), (1,)), ((), ()))


def iota(shape, dim):
    return lax.broadcasted_iota(jnp.int32, shape, dim)


def swap_groups(blocks):
    lane = iota(blocks[0].shape, 1)
    upper = lane >= 64
    odd = (lane // 32) % 2 == 1
    b0, b1, b2, b3 = blocks
    r0, r1, r2, r3 = (pltpu.roll(b, 64, 1) for b in blocks)
    b0, b2 = jnp.where(upper, r2, b0), jnp.where(upper, b2, r0)
    b1, b3 = jnp.where(upper, r3, b1), jnp.where(upper, b3, r1)
    up1, up3 = pltpu.roll(b1, 32, 1), pltpu.roll(b3, 32, 1)
    down0, down2 = pltpu.roll(b0, 96, 1), pltpu.roll(b2, 96, 1)
    return (
        jnp.where(odd, up1, b0),
        jnp.where(odd, b1, down0),
        jnp.where(odd, up3, b2),
        jnp.where(odd, b3, down2),
    )


def choose(condition):
    return condition.astype(F32).astype(BF16)


def channel_lanes():
    lane = iota((32, 512), 1)
    return choose(iota((32, 512), 0) == 4 * ((lane % 128) // 16) + lane // 128)


def own_residue():
    return iota((512, 512), 0) % 16 == iota((512, 512), 1) % 16


def low():
    return iota((8, 128), 1) < 64


def fold(first, second, lower):
    return (
        jnp.where(lower, first, pltpu.roll(second, 64, 1)),
        jnp.where(lower, pltpu.roll(first, 64, 1), second),
    )


def prep_kernel(left_hbm, mask_hbm, out_ref, left_ref, mask_ref, sems):
    copies = [
        pltpu.make_async_copy(left_hbm, left_ref, sems.at[0]),
        pltpu.make_async_copy(mask_hbm, mask_ref, sems.at[1]),
    ]
    for copy in copies:
        copy.start()
    for copy in copies:
        copy.wait()
    spread = jnp.dot(left_ref[...], channel_lanes(), preferred_element_type=F32)
    spread = jnp.where(own_residue(), spread, 0.0).astype(BF16)
    row, col = iota((32, 512), 0), iota((32, 512), 1)
    gather = choose((col // 32 == row % 16) & ((col % 32) // 16 == row // 16))
    block = jnp.dot(gather, spread, preferred_element_type=F32).astype(BF16)
    mask = mask_ref[...].astype(F32).astype(BF16)
    widen = choose(iota((32, 128), 0) == iota((32, 128), 1))
    masks = jnp.dot(mask, widen, preferred_element_type=F32).astype(BF16)
    for r in range(8):
        for h in range(2):
            out_ref[r, :, h * 512 : h * 512 + 512] = block[h * 16 : h * 16 + 16]
        out_ref[r, :, 1024:1152] = masks


def pair_kernel(
    own_ref, other_ref, w_ref, bias_ref, cot_ref,
    pair_ref, send_ref, right_ref, weight_ref, left_ref, bsum_ref,
    y_ref, x_ref, dx_ref, dy_ref, mask_ref, plain_ref, cot32_ref, scaled_ref,
):
    core = lax.axis_index("core")
    keep = pl.multiple_of(core * 512, 512)
    give = pl.multiple_of((1 - core) * 512, 512)

    def rows(lanes):
        return jnp.concatenate([own_ref[:, lanes], other_ref[:, lanes]], 0)

    row, col = iota((256, 256), 0), iota((256, 256), 1)
    device = row % 16
    order = choose(col == ((device + core) % 2) * 128 + (device // 2) * 16 + row // 16)
    masks = jnp.dot(order, rows(slice(2048, 2176)), preferred_element_type=F32).astype(BF16)
    left = jnp.dot(order, rows(pl.ds(keep, 512)), preferred_element_type=F32).astype(BF16)
    right = jnp.dot(order, rows(slice(1024, 2048)), preferred_element_type=F32).astype(BF16)
    lane = iota((128, 512), 1)
    spread_i = choose(iota((128, 512), 0) == core * 16 + lane % 16)
    spread_j = choose(iota((128, 512), 0) == 32 + 4 * ((lane // 16) % 8) + lane // 128)
    spread_jd = choose(iota((128, 1024), 0) == 32 + iota((128, 1024), 1) // 32)
    mask_i = jnp.dot(masks, spread_i, preferred_element_type=F32)
    mask_j = jnp.dot(masks, spread_j, preferred_element_type=F32)
    mask_jd = jnp.dot(masks, spread_jd, preferred_element_type=F32)
    mask_ref[...] = mask_jd
    left = left * mask_i.astype(BF16)
    right = right * mask_jd.astype(BF16)
    both = (mask_i * mask_j).astype(BF16)
    counts = (
        lax.dot_general(both, jnp.ones((256, 128), BF16), ROWS_ROWS, preferred_element_type=F32) + 1e-3
    )
    inverse = 1.0 / counts
    cot32 = cot_ref[...].astype(F32)
    cot32_ref[...] = cot32
    bsum_ref[...] = jnp.sum(cot32, axis=0, keepdims=True)
    for j in range(32):
        at = ((j % 4) * 8 + j // 4) * 16
        scaled_ref[at : at + 16, :] = (
            cot32_ref[pl.ds(j, 16, stride=32), :] * inverse[at : at + 16, :]
        ).astype(BF16)
    scaled = scaled_ref[...]

    y_ref[...] = lax.dot_general(left, right, ROWS_ROWS, preferred_element_type=F32)
    for u in range(8):
        lanes = slice(u * 128, u * 128 + 128)
        for t in range(8):
            tiles = swap_groups([y_ref[f * 128 + t * 16 : f * 128 + t * 16 + 16, lanes] for f in range(4)])
            for e in range(4):
                at = (e * 8 + u) * 16
                x_ref[at : at + 16, t * 128 : t * 128 + 128] = tiles[e].astype(BF16)

    dx_ref[...] = lax.dot_general(scaled, w_ref[...], LANES_LANES, preferred_element_type=F32)
    for u in range(8):
        lanes = slice(u * 128, u * 128 + 128)
        for t in range(8):
            tiles = swap_groups(
                [dx_ref[(e * 8 + u) * 16 : (e * 8 + u) * 16 + 16, t * 128 : t * 128 + 128] for e in range(4)]
            )
            for f in range(4):
                dy_ref[f * 128 + t * 16 : f * 128 + t * 16 + 16, lanes] = tiles[f].astype(BF16)

    def right_part(half):
        part = jnp.dot(left, dy_ref[:, pl.ds(half, 512)], preferred_element_type=F32)
        return part * mask_ref[:, pl.ds(half, 512)]

    def weight_part(half):
        return lax.dot_general(x_ref[:, pl.ds(half, 512)], scaled, ROWS_ROWS, preferred_element_type=F32)

    send_ref[:, 0:512] = right_part(give).astype(BF16)
    part = weight_part(give).astype(BF16)
    send_ref[:, 512:640] = part[0:256]
    send_ref[:, 640:768] = part[256:512]

    right_ref[...] = right_part(keep)
    weight_ref[...] = weight_part(keep)
    left_ref[...] = (
        lax.dot_general(right, dy_ref[...], LANES_LANES, preferred_element_type=F32) * mask_i
    )
    update = jnp.dot(x_ref[...], w_ref[...], preferred_element_type=F32) * inverse + bias_ref[...]
    for j in range(32):
        at = ((j % 4) * 8 + j // 4) * 16
        plain_ref[pl.ds(j, 16, stride=32), :] = update[at : at + 16, :]
    pair_ref[...] = plain_ref[...].astype(BF16)


def pack_kernel(got_ref, right_ref, weight_ref, left_ref, msg_ref):
    lower = low()
    upper_rows = iota((8, 128), 0) >= 4
    for s in range(16):
        for k in range(4):
            m = s * 8 + k * 2
            lanes = slice(k * 128, k * 128 + 128)
            total = right_ref[s * 16 : s * 16 + 16, lanes] + got_ref[s * 16 : s * 16 + 16, lanes].astype(F32)
            tiles = []
            for block in (total, left_ref[s * 16 : s * 16 + 16, lanes]):
                even, odd = fold(block[0:8], block[8:16], lower)
                tiles.append(jnp.where(upper_rows, pltpu.roll(odd, 4, 0), even))
                tiles.append(jnp.where(upper_rows, odd, pltpu.roll(even, 4, 0)))
            at = (m // 2) * 8
            side = slice(512 + (at // 256) * 128, 640 + (at // 256) * 128)
            first = at % 256 // 16 * 16
            got = got_ref[first : first + 16, side].astype(F32)
            tiles.append(weight_ref[at : at + 8, :] + got[at % 16 : at % 16 + 8])
            for n in range(5):
                tile = tiles[n].astype(BF16)
                msg_ref[m, :, n * 128 : n * 128 + 128] = tile[0:4]
                msg_ref[m + 1, :, n * 128 : n * 128 + 128] = tile[4:8]


def reduce_kernel(in_ref, bsum_ref, out_ref, rows_ref):
    lower = iota((4, 128), 1) < 64
    weight = [jnp.zeros((4, 128), F32) for core in range(2)]
    left = [jnp.zeros((4, 256), F32) for q in range(16)]

    def spread(parts, owner, row):
        for b in range(2):
            lanes = slice(b * 128, b * 128 + 128)
            near, far = fold(parts[0][:, lanes], parts[1][:, lanes], lower)
            rows_ref[pl.ds(b * 256 + owner * 8 + row, 4, stride=64), :] = near
            rows_ref[pl.ds(512 + b * 256 + owner * 8 + row, 4, stride=64), :] = far

    for r in range(8):
        right = []
        for core in range(2):
            total = jnp.zeros((4, 256), F32)
            for chip in range(8):
                q = chip * 2 + core
                block = in_ref[q * 8 + r].astype(F32)
                total = total + block[:, 0:256]
                left[q] = left[q] + block[:, 256:512]
                weight[core] = weight[core] + block[:, 512:640]
            right.append(total)
        spread(right, r, 4)
    for chip in range(8):
        spread(left[chip * 2 : chip * 2 + 2], chip, 5)
    bias = bsum_ref[...]
    high = bias.astype(BF16).astype(F32)
    tail = [jnp.zeros((2, 128), F32), high, bias - high]
    base = [jnp.concatenate([weight[core]] + tail, 0) for core in range(2)]
    sub = iota((8, 128), 0)
    mine = (sub == 4) | (sub == 5)
    for m in range(128):
        rows = rows_ref[m * 8 : m * 8 + 8, :]
        out_ref[m] = jnp.where(mine, rows, base[(m // 8) % 2]).astype(BF16)


def operand_kernel(in_ref, right_ref, left_ref, bias_ref, rows_ref):
    lower = iota((16, 128), 1) < 64
    total = jnp.zeros((8, 128), F32)
    for m in range(128):
        block = in_ref[m].astype(F32)
        rows_ref[m * 8 : m * 8 + 8, :] = block
        total = total + block
    bias_ref[...] = total[6:7] + total[7:8]

    def tiles(row):
        pairs = [
            fold(
                rows_ref[pl.ds(k * 16 + row, 16, stride=64), :],
                rows_ref[pl.ds(k * 16 + 8 + row, 16, stride=64), :],
                lower,
            )
            for k in range(4)
        ]
        return [p[0] for p in pairs], [p[1] for p in pairs]

    near, far = tiles(4)
    for k, tile in enumerate(near + far):
        for e in range(4):
            right_ref[pl.ds(k * 4 + e, 16, stride=32), :] = tile[:, e * 32 : e * 32 + 32]
    near, far = tiles(5)
    left = jnp.concatenate([jnp.concatenate(near, 1), jnp.concatenate(far, 1)], 0).astype(BF16)
    row, col = iota((512, 32), 0), iota((512, 32), 1)
    scatter = choose((row // 32 == col % 16) & ((row % 32) // 16 == col // 16))
    spread = jnp.dot(scatter, left, preferred_element_type=F32)
    spread = jnp.where(own_residue(), spread, 0.0).astype(BF16)
    left_ref[...] = lax.dot_general(spread, channel_lanes(), LANES_LANES, preferred_element_type=F32)


def weight_kernel(own_ref, other_ref, out_ref):
    core = lax.axis_index("core")
    upper_rows = iota((8, 128), 0) >= 4
    for p in range(64):
        for ref, half in ((own_ref, core), (other_ref, 1 - core)):
            even, odd = ref[p * 2].astype(F32), ref[p * 2 + 1].astype(F32)
            at = pl.multiple_of(half * 512 + p * 8, 8)
            out_ref[pl.ds(at, 8), :] = jnp.where(upper_rows, pltpu.roll(odd, 4, 0), even)


def call(kernel, outs, scratch, *args, space=pltpu.VMEM, mib=40):
    whole = pl.BlockSpec(memory_space=pltpu.VMEM)
    return pl.pallas_call(
        kernel,
        out_shape=outs,
        in_specs=[pl.BlockSpec(memory_space=space)] * len(args),
        out_specs=tuple([whole] * len(outs)),
        scratch_shapes=scratch,
        compiler_params=pltpu.CompilerParams(vmem_limit_bytes=mib * 1024 * 1024),
    )(*args)


def shape(dims, dtype):
    return jax.ShapeDtypeStruct(dims, dtype)


def per_device(left, right, mask, weight, bias, cotangent):
    swap = [(0, 1), (1, 0)]
    devices = ("chip", "core", "res")
    (block,) = call(
        prep_kernel,
        (shape((8, 16, 1152), BF16),),
        [pltpu.VMEM((512, 32), BF16), pltpu.VMEM((16, 32), jnp.int32), pltpu.SemaphoreType.DMA((2,))],
        left.reshape(512, 32),
        mask,
        space=pltpu.HBM,
        mib=60,
    )
    block = lax.all_to_all(block, "res", 0, 0, tiled=True)
    block, right, mask = lax.optimization_barrier((block, right, mask))
    masks = jnp.pad(mask.astype(BF16), ((0, 0), (32, 64)))
    rights = jnp.broadcast_to(right.reshape(16, 1024), (8, 16, 1024))
    block = jnp.concatenate([block[:, :, :1024], rights, block[:, :, 1024:] + masks], -1)
    own = lax.all_to_all(block, "chip", 0, 0, tiled=True).reshape(128, 2176)
    other = lax.ppermute(own, "core", swap)

    pair_update, send, right_part, weight_part, left_part, bias_part = call(
        pair_kernel,
        (
            shape((512, 128), BF16),
            shape((256, 768), BF16),
            shape((256, 512), F32),
            shape((512, 128), F32),
            shape((256, 512), F32),
            shape((1, 128), F32),
        ),
        [
            pltpu.VMEM((512, 1024), F32),
            pltpu.VMEM((512, 1024), BF16),
            pltpu.VMEM((512, 1024), F32),
            pltpu.VMEM((512, 1024), BF16),
            pltpu.VMEM((256, 1024), F32),
            pltpu.VMEM((512, 128), F32),
            pltpu.VMEM((512, 128), F32),
            pltpu.VMEM((512, 128), BF16),
        ],
        own,
        other,
        weight.reshape(1024, 128),
        bias.reshape(1, 128),
        cotangent.reshape(512, 128),
    )
    got = lax.ppermute(send, "core", swap)
    (parts,) = call(
        pack_kernel,
        (shape((128, 4, 640), BF16),),
        [],
        got,
        right_part,
        weight_part,
        left_part,
    )
    parts = lax.all_to_all(parts, devices, 0, 0, tiled=True)
    (sums,) = call(
        reduce_kernel, (shape((128, 8, 128), BF16),), [pltpu.VMEM((1024, 128), F32)], parts, bias_part
    )
    sums = lax.all_to_all(sums, devices, 0, 0, tiled=True)
    other_sums = lax.ppermute(sums, "core", swap)
    right_grad, left_grad, bias_grad = call(
        operand_kernel,
        (shape((512, 32), F32), shape((512, 32), F32), shape((1, 128), F32)),
        [pltpu.VMEM((1024, 128), F32)],
        sums,
    )
    (weight_grad,) = call(weight_kernel, (shape((1024, 128), F32),), [], sums, other_sums)
    return (
        pair_update.reshape(16, 32, 128),
        left_grad.reshape(16, 32, 32),
        right_grad.reshape(16, 32, 32),
        weight_grad.reshape(32, 32, 128),
        bias_grad.reshape(128),
    )


def solution(mesh):
    mesh = Mesh(mesh.devices.reshape(8, 2, 8), ("chip", "core", "res"))
    seq = ("chip", "core")
    return jax.shard_map(
        per_device,
        mesh=mesh,
        in_specs=(
            P(seq, "res", None),
            P(seq, "res", None),
            P(seq, "res"),
            P(),
            P(),
            P(seq, "res", None),
        ),
        out_specs=(P(seq, "res", None), P(seq, "res", None), P(seq, "res", None), P(), P()),
        check_vma=False,
    )
```

```python
import jax
import jax.numpy as jnp
from jax import lax
from jax.experimental import pallas as pl
from jax.experimental.pallas import tpu as pltpu
from jax.sharding import Mesh
from jax.sharding import PartitionSpec as P

F32 = jnp.float32
BF16 = jnp.bfloat16
ROWS_ROWS = (((0,), (0,)), ((), ()))
LANES_LANES = (((1,), (1,)), ((), ()))


def iota(shape, dim):
    return lax.broadcasted_iota(jnp.int32, shape, dim)


def swap_groups(blocks):
    lane = iota(blocks[0].shape, 1)
    upper = lane >= 64
    odd = (lane // 32) % 2 == 1
    b0, b1, b2, b3 = blocks
    r0, r1, r2, r3 = (pltpu.roll(b, 64, 1) for b in blocks)
    b0, b2 = jnp.where(upper, r2, b0), jnp.where(upper, b2, r0)
    b1, b3 = jnp.where(upper, r3, b1), jnp.where(upper, b3, r1)
    up1, up3 = pltpu.roll(b1, 32, 1), pltpu.roll(b3, 32, 1)
    down0, down2 = pltpu.roll(b0, 96, 1), pltpu.roll(b2, 96, 1)
    return (
        jnp.where(odd, up1, b0),
        jnp.where(odd, b1, down0),
        jnp.where(odd, up3, b2),
        jnp.where(odd, b3, down2),
    )


def choose(condition):
    return condition.astype(F32).astype(BF16)


def channel_lanes():
    lane = iota((32, 512), 1)
    return choose(iota((32, 512), 0) == 4 * ((lane % 128) // 16) + lane // 128)


def own_residue():
    return iota((512, 512), 0) % 16 == iota((512, 512), 1) % 16


def low():
    return iota((8, 128), 1) < 64


def fold(first, second, lower):
    return (
        jnp.where(lower, first, pltpu.roll(second, 64, 1)),
        jnp.where(lower, pltpu.roll(first, 64, 1), second),
    )


def prep_kernel(
    left_hbm, right_hbm, mask_hbm, left_out, right_out, left_ref, right_ref, mask_ref, right32_ref, sems
):
    copies = [
        pltpu.make_async_copy(left_hbm, left_ref, sems.at[0]),
        pltpu.make_async_copy(right_hbm, right_ref, sems.at[1]),
        pltpu.make_async_copy(mask_hbm, mask_ref, sems.at[2]),
    ]
    for copy in copies:
        copy.start()
    for copy in copies:
        copy.wait()
    spread = jnp.dot(left_ref[...], channel_lanes(), preferred_element_type=F32)
    spread = jnp.where(own_residue(), spread, 0.0).astype(BF16)
    row, col = iota((32, 512), 0), iota((32, 512), 1)
    gather = choose((col // 32 == row % 16) & ((col % 32) // 16 == row // 16))
    block = jnp.dot(gather, spread, preferred_element_type=F32).astype(BF16)
    mask = mask_ref[...].astype(F32).astype(BF16)
    row, col = iota((32, 128), 0), iota((32, 128), 1)
    masks = jnp.dot(mask, choose(row == col), preferred_element_type=F32).astype(BF16)
    for r in range(8):
        for h in range(2):
            left_out[r, :, h * 512 : h * 512 + 512] = block[h * 16 : h * 16 + 16]
        left_out[r, :, 1024:1152] = masks
    right32_ref[...] = right_ref[...].astype(F32)
    for k in range(8):
        tile = [right32_ref[pl.ds(k * 4 + e, 16, stride=32), :] for e in range(4)]
        right_out[:, k * 128 : k * 128 + 128] = jnp.concatenate(tile, 1).astype(BF16)
    right_out[:, 1024:1152] = jnp.dot(mask, choose(row + 32 == col), preferred_element_type=F32).astype(BF16)


def outer_kernel(
    own_ref, other_ref, w_ref, cot_ref,
    send_ref, x_ref, dy_ref, left_ref, right_ref, mask_i_ref, mask_jd_ref, scaled_ref, inverse_ref, bsum_ref,
    y_ref, dx_ref, cot32_ref,
):
    core = lax.axis_index("core")
    keep = pl.multiple_of(core * 512, 512)
    give = pl.multiple_of((1 - core) * 512, 512)

    def rows(lanes):
        return jnp.concatenate([own_ref[:, lanes], other_ref[:, lanes]], 0)

    row, col = iota((256, 256), 0), iota((256, 256), 1)
    device = row % 16
    order = choose(col == ((device + core) % 2) * 128 + (device // 2) * 16 + row // 16)
    masks = jnp.dot(order, rows(slice(2048, 2176)), preferred_element_type=F32).astype(BF16)
    left = jnp.dot(order, rows(pl.ds(keep, 512)), preferred_element_type=F32).astype(BF16)
    right = jnp.dot(order, rows(slice(1024, 2048)), preferred_element_type=F32).astype(BF16)
    lane = iota((128, 512), 1)
    spread_i = choose(iota((128, 512), 0) == core * 16 + lane % 16)
    spread_j = choose(iota((128, 512), 0) == 32 + 4 * ((lane // 16) % 8) + lane // 128)
    spread_jd = choose(iota((128, 1024), 0) == 32 + iota((128, 1024), 1) // 32)
    mask_i = jnp.dot(masks, spread_i, preferred_element_type=F32)
    mask_j = jnp.dot(masks, spread_j, preferred_element_type=F32)
    mask_jd = jnp.dot(masks, spread_jd, preferred_element_type=F32)
    mask_i_ref[...] = mask_i.astype(BF16)
    mask_jd_ref[...] = mask_jd.astype(BF16)
    left = left * mask_i_ref[...]
    right = right * mask_jd_ref[...]
    left_ref[...] = left
    right_ref[...] = right
    both = (mask_i * mask_j).astype(BF16)
    counts = (
        lax.dot_general(both, jnp.ones((256, 128), BF16), ROWS_ROWS, preferred_element_type=F32) + 1e-3
    )
    inverse = 1.0 / counts
    inverse_ref[...] = inverse
    cot32 = cot_ref[...].astype(F32)
    cot32_ref[...] = cot32
    bsum_ref[...] = jnp.sum(cot32, axis=0, keepdims=True)
    for j in range(32):
        at = ((j % 4) * 8 + j // 4) * 16
        scaled_ref[at : at + 16, :] = (
            cot32_ref[pl.ds(j, 16, stride=32), :] * inverse[at : at + 16, :]
        ).astype(BF16)
    scaled = scaled_ref[...]

    y_ref[...] = lax.dot_general(left, right, ROWS_ROWS, preferred_element_type=F32)
    for u in range(8):
        lanes = slice(u * 128, u * 128 + 128)
        for t in range(8):
            tiles = swap_groups([y_ref[f * 128 + t * 16 : f * 128 + t * 16 + 16, lanes] for f in range(4)])
            for e in range(4):
                at = (e * 8 + u) * 16
                x_ref[at : at + 16, t * 128 : t * 128 + 128] = tiles[e].astype(BF16)

    dx_ref[...] = lax.dot_general(scaled, w_ref[...], LANES_LANES, preferred_element_type=F32)
    for u in range(8):
        lanes = slice(u * 128, u * 128 + 128)
        for t in range(8):
            tiles = swap_groups(
                [dx_ref[(e * 8 + u) * 16 : (e * 8 + u) * 16 + 16, t * 128 : t * 128 + 128] for e in range(4)]
            )
            for f in range(4):
                dy_ref[f * 128 + t * 16 : f * 128 + t * 16 + 16, lanes] = tiles[f].astype(BF16)

    part = right_part(give, left, dy_ref, mask_jd_ref).astype(BF16)
    send_ref[:, 0:512] = part
    part = weight_part(give, x_ref, scaled).astype(BF16)
    send_ref[:, 512:640] = part[0:256]
    send_ref[:, 640:768] = part[256:512]


def right_part(half, left, dy_ref, mask_ref):
    part = jnp.dot(left, dy_ref[:, pl.ds(half, 512)], preferred_element_type=F32)
    return part * mask_ref[:, pl.ds(half, 512)].astype(F32)


def weight_part(half, x_ref, scaled):
    return lax.dot_general(x_ref[:, pl.ds(half, 512)], scaled, ROWS_ROWS, preferred_element_type=F32)


def sums_kernel(
    x_ref, dy_ref, left_in, right_in, mask_i_ref, mask_jd_ref, scaled_ref, inverse_ref, w_ref, bias_ref,
    update_ref, right_ref, weight_ref, left_ref,
):
    keep = pl.multiple_of(lax.axis_index("core") * 512, 512)
    right_ref[...] = right_part(keep, left_in[...], dy_ref, mask_jd_ref)
    weight_ref[...] = weight_part(keep, x_ref, scaled_ref[...])
    left = lax.dot_general(right_in[...], dy_ref[...], LANES_LANES, preferred_element_type=F32)
    left_ref[...] = left * mask_i_ref[...].astype(F32)
    update_ref[...] = (
        jnp.dot(x_ref[...], w_ref[...], preferred_element_type=F32) * inverse_ref[...] + bias_ref[...]
    )


def pack_kernel(got_ref, right_ref, weight_ref, left_ref, msg_ref):
    lower = low()
    upper_rows = iota((8, 128), 0) >= 4
    for s in range(16):
        for k in range(4):
            m = s * 8 + k * 2
            lanes = slice(k * 128, k * 128 + 128)
            total = right_ref[s * 16 : s * 16 + 16, lanes] + got_ref[s * 16 : s * 16 + 16, lanes].astype(F32)
            tiles = []
            for block in (total, left_ref[s * 16 : s * 16 + 16, lanes]):
                even, odd = fold(block[0:8], block[8:16], lower)
                tiles.append(jnp.where(upper_rows, pltpu.roll(odd, 4, 0), even))
                tiles.append(jnp.where(upper_rows, odd, pltpu.roll(even, 4, 0)))
            at = (m // 2) * 8
            side = slice(512 + (at // 256) * 128, 640 + (at // 256) * 128)
            first = at % 256 // 16 * 16
            got = got_ref[first : first + 16, side].astype(F32)
            tiles.append(weight_ref[at : at + 8, :] + got[at % 16 : at % 16 + 8])
            for n in range(5):
                tile = tiles[n].astype(BF16)
                msg_ref[m, :, n * 128 : n * 128 + 128] = tile[0:4]
                msg_ref[m + 1, :, n * 128 : n * 128 + 128] = tile[4:8]


def reduce_kernel(in_ref, bsum_ref, out_ref, rows_ref):
    lower = iota((4, 128), 1) < 64
    weight = [jnp.zeros((4, 128), F32) for core in range(2)]
    left = [jnp.zeros((4, 256), F32) for q in range(16)]

    def spread(parts, owner, row):
        for b in range(2):
            lanes = slice(b * 128, b * 128 + 128)
            near, far = fold(parts[0][:, lanes], parts[1][:, lanes], lower)
            rows_ref[pl.ds(b * 256 + owner * 8 + row, 4, stride=64), :] = near
            rows_ref[pl.ds(512 + b * 256 + owner * 8 + row, 4, stride=64), :] = far

    for r in range(8):
        right = []
        for core in range(2):
            total = jnp.zeros((4, 256), F32)
            for chip in range(8):
                q = chip * 2 + core
                block = in_ref[q * 8 + r].astype(F32)
                total = total + block[:, 0:256]
                left[q] = left[q] + block[:, 256:512]
                weight[core] = weight[core] + block[:, 512:640]
            right.append(total)
        spread(right, r, 4)
    for chip in range(8):
        spread(left[chip * 2 : chip * 2 + 2], chip, 5)
    bias = bsum_ref[...]
    high = bias.astype(BF16).astype(F32)
    tail = [jnp.zeros((2, 128), F32), high, bias - high]
    base = [jnp.concatenate([weight[core]] + tail, 0) for core in range(2)]
    sub = iota((8, 128), 0)
    mine = (sub == 4) | (sub == 5)
    for m in range(128):
        rows = rows_ref[m * 8 : m * 8 + 8, :]
        out_ref[m] = jnp.where(mine, rows, base[(m // 8) % 2]).astype(BF16)


def weight_rows(ref, out_ref):
    upper_rows = iota((8, 128), 0) >= 4
    for p in range(64):
        even, odd = ref[p * 2].astype(F32), ref[p * 2 + 1].astype(F32)
        out_ref[p * 8 : p * 8 + 8, :] = jnp.where(upper_rows, pltpu.roll(odd, 4, 0), even)


def operand_kernel(
    in_ref, update_ref, pair_ref, right_ref, left_ref, bias_ref, rows_ref, plain_ref
):
    for j in range(32):
        at = ((j % 4) * 8 + j // 4) * 16
        plain_ref[pl.ds(j, 16, stride=32), :] = update_ref[at : at + 16, :]
    pair_ref[...] = plain_ref[...].astype(BF16)
    lower = iota((16, 128), 1) < 64
    total = jnp.zeros((8, 128), F32)
    for m in range(128):
        block = in_ref[m].astype(F32)
        rows_ref[m * 8 : m * 8 + 8, :] = block
        total = total + block
    bias_ref[...] = total[6:7] + total[7:8]

    def tiles(row):
        pairs = [
            fold(
                rows_ref[pl.ds(k * 16 + row, 16, stride=64), :],
                rows_ref[pl.ds(k * 16 + 8 + row, 16, stride=64), :],
                lower,
            )
            for k in range(4)
        ]
        return [p[0] for p in pairs], [p[1] for p in pairs]

    near, far = tiles(4)
    for k, tile in enumerate(near + far):
        for e in range(4):
            right_ref[pl.ds(k * 4 + e, 16, stride=32), :] = tile[:, e * 32 : e * 32 + 32]
    near, far = tiles(5)
    left = jnp.concatenate([jnp.concatenate(near, 1), jnp.concatenate(far, 1)], 0).astype(BF16)
    row, col = iota((512, 32), 0), iota((512, 32), 1)
    scatter = choose((row // 32 == col % 16) & ((row % 32) // 16 == col // 16))
    spread = jnp.dot(scatter, left, preferred_element_type=F32)
    spread = jnp.where(own_residue(), spread, 0.0).astype(BF16)
    left_ref[...] = lax.dot_general(spread, channel_lanes(), LANES_LANES, preferred_element_type=F32)


def weight_kernel(own_ref, other_ref, out_hbm, rows_ref, sems):
    core = lax.axis_index("core")
    copies = []
    for n, (ref, half) in enumerate(((own_ref, core), (other_ref, 1 - core))):
        weight_rows(ref, rows_ref.at[n])
        at = pl.ds(pl.multiple_of(half * 512, 512), 512)
        copies.append(pltpu.make_async_copy(rows_ref.at[n], out_hbm.at[at], sems.at[n]))
        copies[n].start()
    for copy in copies:
        copy.wait()


def call(kernel, outs, scratch, *args, space=pltpu.VMEM, mib=40, out_space=pltpu.VMEM):
    return pl.pallas_call(
        kernel,
        out_shape=outs,
        in_specs=[pl.BlockSpec(memory_space=space)] * len(args),
        out_specs=tuple([pl.BlockSpec(memory_space=out_space)] * len(outs)),
        scratch_shapes=scratch,
        compiler_params=pltpu.CompilerParams(vmem_limit_bytes=mib * 1024 * 1024),
    )(*args)


def shape(dims, dtype):
    return jax.ShapeDtypeStruct(dims, dtype)


def per_device(left, right, mask, weight, bias, cotangent):
    swap = [(0, 1), (1, 0)]
    devices = ("chip", "core", "res")
    block, rights = call(
        prep_kernel,
        (shape((8, 16, 1152), BF16), shape((16, 1152), BF16)),
        [
            pltpu.VMEM((512, 32), BF16),
            pltpu.VMEM((512, 32), BF16),
            pltpu.VMEM((16, 32), jnp.int32),
            pltpu.VMEM((512, 32), F32),
            pltpu.SemaphoreType.DMA((3,)),
        ],
        left.reshape(512, 32),
        right.reshape(512, 32),
        mask,
        space=pltpu.HBM,
        mib=60,
    )
    block = lax.all_to_all(block, "res", 0, 0, tiled=True)
    rights = jnp.broadcast_to(rights, (8, 16, 1152))
    block = jnp.concatenate(
        [block[..., :1024], rights[..., :1024], block[..., 1024:] + rights[..., 1024:]], -1
    )
    own = lax.all_to_all(block, "chip", 0, 0, tiled=True).reshape(128, 2176)
    other = lax.ppermute(own, "core", swap)

    weight = weight.reshape(1024, 128)
    send, outer, outer_grad, left_all, right_all, mask_i, mask_jd, scaled, inverse, bias_part = call(
        outer_kernel,
        (
            shape((256, 768), BF16),
            shape((512, 1024), BF16),
            shape((512, 1024), BF16),
            shape((256, 512), BF16),
            shape((256, 1024), BF16),
            shape((256, 512), BF16),
            shape((256, 1024), BF16),
            shape((512, 128), BF16),
            shape((512, 128), F32),
            shape((1, 128), F32),
        ),
        [pltpu.VMEM((512, 1024), F32), pltpu.VMEM((512, 1024), F32), pltpu.VMEM((512, 128), F32)],
        own,
        other,
        weight,
        cotangent.reshape(512, 128),
    )
    got = lax.ppermute(send, "core", swap)
    update, right_sum, weight_sum, left_sum = call(
        sums_kernel,
        (shape((512, 128), F32), shape((256, 512), F32), shape((512, 128), F32), shape((256, 512), F32)),
        [],
        outer,
        outer_grad,
        left_all,
        right_all,
        mask_i,
        mask_jd,
        scaled,
        inverse,
        weight,
        bias.reshape(1, 128),
    )
    (parts,) = call(
        pack_kernel,
        (shape((128, 4, 640), BF16),),
        [],
        got,
        right_sum,
        weight_sum,
        left_sum,
    )
    parts = lax.all_to_all(parts, devices, 0, 0, tiled=True)
    (sums,) = call(
        reduce_kernel, (shape((128, 8, 128), BF16),), [pltpu.VMEM((1024, 128), F32)], parts, bias_part
    )
    sums = lax.all_to_all(sums, devices, 0, 0, tiled=True)
    other_sums = lax.ppermute(sums, "core", swap)
    pair_update, right_grad, left_grad, bias_grad = call(
        operand_kernel,
        (shape((512, 128), BF16), shape((512, 32), F32), shape((512, 32), F32), shape((1, 128), F32)),
        [pltpu.VMEM((1024, 128), F32), pltpu.VMEM((512, 128), F32)],
        sums,
        update,
    )
    (weight_grad,) = call(
        weight_kernel,
        (shape((1024, 128), F32),),
        [pltpu.VMEM((2, 512, 128), F32), pltpu.SemaphoreType.DMA((2,))],
        sums,
        other_sums,
        out_space=pltpu.HBM,
    )
    return (
        pair_update.reshape(16, 32, 128),
        left_grad.reshape(16, 32, 32),
        right_grad.reshape(16, 32, 32),
        weight_grad.reshape(32, 32, 128),
        bias_grad.reshape(128),
    )


def solution(mesh):
    mesh = Mesh(mesh.devices.reshape(8, 2, 8), ("chip", "core", "res"))
    seq = ("chip", "core")
    return jax.shard_map(
        per_device,
        mesh=mesh,
        in_specs=(
            P(seq, "res", None),
            P(seq, "res", None),
            P(seq, "res"),
            P(),
            P(),
            P(seq, "res", None),
        ),
        out_specs=(P(seq, "res", None), P(seq, "res", None), P(seq, "res", None), P(), P()),
        check_vma=False,
    )
```

```python
import jax
import jax.numpy as jnp
import numpy as np
from jax import lax
from jax.experimental import pallas as pl
from jax.experimental.pallas import tpu as pltpu
from jax.sharding import PartitionSpec as P

F32 = jnp.float32
BF16 = jnp.bfloat16
DEVICES = ("seq", "res")
ROWS_ROWS = (((0,), (0,)), ((), ()))
LANES_LANES = (((1,), (1,)), ((), ()))


def iota(shape, dim):
    return lax.broadcasted_iota(jnp.int32, shape, dim)


def swap_groups(blocks):
    lane = iota(blocks[0].shape, 1)
    upper = lane >= 64
    odd = (lane // 32) % 2 == 1
    b0, b1, b2, b3 = blocks
    r0, r1, r2, r3 = (pltpu.roll(b, 64, 1) for b in blocks)
    b0, b2 = jnp.where(upper, r2, b0), jnp.where(upper, b2, r0)
    b1, b3 = jnp.where(upper, r3, b1), jnp.where(upper, b3, r1)
    up1, up3 = pltpu.roll(b1, 32, 1), pltpu.roll(b3, 32, 1)
    down0, down2 = pltpu.roll(b0, 96, 1), pltpu.roll(b2, 96, 1)
    return (
        jnp.where(odd, up1, b0),
        jnp.where(odd, b1, down0),
        jnp.where(odd, up3, b2),
        jnp.where(odd, b3, down2),
    )


def choose(condition):
    return condition.astype(F32).astype(BF16)


def lane_order():
    lane = np.arange(512)
    source = (lane % 16) * 32 + 4 * ((lane % 128) // 16) + lane // 128
    return jnp.asarray(np.arange(512)[:, None] == source[None, :], BF16)


def core_index():
    return lax.axis_index("seq") % 2


def low():
    return iota((8, 128), 1) < 64


def fold(first, second, lower):
    return (
        jnp.where(lower, first, pltpu.roll(second, 64, 1)),
        jnp.where(lower, pltpu.roll(first, 64, 1), second),
    )


def prep_kernel(
    left_hbm, right_hbm, mask_hbm, left_out, right_out, left_ref, right_ref, mask_ref, wide_ref, sems
):
    copies = [
        pltpu.make_async_copy(left_hbm, left_ref, sems.at[0]),
        pltpu.make_async_copy(right_hbm, right_ref, sems.at[1]),
        pltpu.make_async_copy(mask_hbm, mask_ref, sems.at[2]),
    ]
    for copy in copies:
        copy.start()
    for copy in copies:
        copy.wait()
    mask = mask_ref[...].astype(F32).astype(BF16)
    widen = choose(iota((32, 128), 0) == iota((32, 128), 1))
    masks = jnp.dot(mask, widen, preferred_element_type=F32).astype(BF16)
    for n, (ref, out_ref) in enumerate(((left_ref, left_out), (right_ref, right_out))):
        wide_ref[n] = ref[...].astype(F32)
        for k in range(8):
            tile = [wide_ref[n, pl.ds(k * 4 + e, 16, stride=32), :] for e in range(4)]
            out_ref[:, k * 128 : k * 128 + 128] = jnp.concatenate(tile, 1).astype(BF16)
        out_ref[:, 1024:1152] = masks


def outer_kernel(
    own_ref, other_ref, lanes_ref, w_ref, cot_ref,
    send_ref, x_ref, dy_ref, left_ref, right_ref, mask_i_ref, mask_jd_ref, scaled_ref, inverse_ref, bsum_ref,
    y_ref, dx_ref, cot32_ref,
):
    core = core_index()
    keep = pl.multiple_of(core * 512, 512)
    give = pl.multiple_of((1 - core) * 512, 512)

    def rows(lanes, of_left):
        return jnp.where(core == (0 if of_left else 1), own_ref[:, lanes], other_ref[:, lanes])

    row, col = iota((256, 256), 0), iota((256, 256), 1)
    device = row % 16
    left_order = choose(col == ((device // 2 + 4) % 8) * 32 + (device % 2) * 16 + row // 16)
    right_order = choose(col == (device // 2) * 32 + (1 - device % 2) * 16 + row // 16)

    def ordered(order, block):
        return jnp.dot(order, block, preferred_element_type=F32).astype(BF16)

    masks = ordered(left_order, rows(slice(1024, 1152), True))
    left = ordered(ordered(left_order, rows(pl.ds(keep, 512), True)), lanes_ref[...])
    right = ordered(right_order, rows(slice(0, 1152), False))
    lane = iota((128, 512), 1)
    spread_i = choose(iota((128, 512), 0) == core * 16 + lane % 16)
    spread_j = choose(iota((128, 512), 0) == 4 * ((lane // 16) % 8) + lane // 128)
    spread_jd = choose(iota((128, 1024), 0) == iota((128, 1024), 1) // 32)
    masks_j = right[:, 1024:1152]
    mask_i = jnp.dot(masks, spread_i, preferred_element_type=F32)
    mask_j = jnp.dot(masks_j, spread_j, preferred_element_type=F32)
    mask_jd = jnp.dot(masks_j, spread_jd, preferred_element_type=F32)
    mask_i_ref[...] = mask_i.astype(BF16)
    mask_jd_ref[...] = mask_jd.astype(BF16)
    left = left * mask_i_ref[...]
    right = right[:, 0:1024] * mask_jd_ref[...]
    left_ref[...] = left
    right_ref[...] = right
    both = (mask_i * mask_j).astype(BF16)
    counts = (
        lax.dot_general(both, jnp.ones((256, 128), BF16), ROWS_ROWS, preferred_element_type=F32) + 1e-3
    )
    inverse = 1.0 / counts
    inverse_ref[...] = inverse
    cot32 = cot_ref[...].astype(F32)
    cot32_ref[...] = cot32
    bsum_ref[...] = jnp.sum(cot32, axis=0, keepdims=True)
    for j in range(32):
        at = ((j % 4) * 8 + j // 4) * 16
        scaled_ref[at : at + 16, :] = (
            cot32_ref[pl.ds(j, 16, stride=32), :] * inverse[at : at + 16, :]
        ).astype(BF16)
    scaled = scaled_ref[...]

    y_ref[...] = lax.dot_general(left, right, ROWS_ROWS, preferred_element_type=F32)
    for u in range(8):
        lanes = slice(u * 128, u * 128 + 128)
        for t in range(8):
            tiles = swap_groups([y_ref[f * 128 + t * 16 : f * 128 + t * 16 + 16, lanes] for f in range(4)])
            for e in range(4):
                at = (e * 8 + u) * 16
                x_ref[at : at + 16, t * 128 : t * 128 + 128] = tiles[e].astype(BF16)

    dx_ref[...] = lax.dot_general(scaled, w_ref[...], LANES_LANES, preferred_element_type=F32)
    for u in range(8):
        lanes = slice(u * 128, u * 128 + 128)
        for t in range(8):
            tiles = swap_groups(
                [dx_ref[(e * 8 + u) * 16 : (e * 8 + u) * 16 + 16, t * 128 : t * 128 + 128] for e in range(4)]
            )
            for f in range(4):
                dy_ref[f * 128 + t * 16 : f * 128 + t * 16 + 16, lanes] = tiles[f].astype(BF16)

    part = right_part(give, left, dy_ref, mask_jd_ref).astype(BF16)
    send_ref[:, 0:512] = part
    part = weight_part(give, x_ref, scaled).astype(BF16)
    send_ref[:, 512:640] = part[0:256]
    send_ref[:, 640:768] = part[256:512]


def right_part(half, left, dy_ref, mask_ref):
    part = jnp.dot(left, dy_ref[:, pl.ds(half, 512)], preferred_element_type=F32)
    return part * mask_ref[:, pl.ds(half, 512)].astype(F32)


def weight_part(half, x_ref, scaled):
    return lax.dot_general(x_ref[:, pl.ds(half, 512)], scaled, ROWS_ROWS, preferred_element_type=F32)


def sums_kernel(
    x_ref, dy_ref, left_in, right_in, mask_i_ref, mask_jd_ref, scaled_ref, inverse_ref, lanes_ref, w_ref, bias_ref,
    update_ref, right_ref, weight_ref, left_ref,
):
    keep = pl.multiple_of(core_index() * 512, 512)
    right_ref[...] = right_part(keep, left_in[...], dy_ref, mask_jd_ref)
    weight_ref[...] = weight_part(keep, x_ref, scaled_ref[...])
    left = lax.dot_general(right_in[...], dy_ref[...], LANES_LANES, preferred_element_type=F32)
    left = (left * mask_i_ref[...].astype(F32)).astype(BF16)
    left_ref[...] = lax.dot_general(left, lanes_ref[...], LANES_LANES, preferred_element_type=F32)
    update_ref[...] = (
        jnp.dot(x_ref[...], w_ref[...], preferred_element_type=F32) * inverse_ref[...] + bias_ref[0:1, :]
    )


def pack_kernel(got_ref, right_ref, weight_ref, left_ref, msg_ref):
    lower = low()
    upper_rows = iota((8, 128), 0) >= 4
    for s in range(16):
        for k in range(4):
            m = s * 8 + k * 2
            lanes = slice(k * 128, k * 128 + 128)
            total = right_ref[s * 16 : s * 16 + 16, lanes] + got_ref[s * 16 : s * 16 + 16, lanes].astype(F32)
            tiles = []
            for block in (total, left_ref[s * 16 : s * 16 + 16, lanes]):
                even, odd = fold(block[0:8], block[8:16], lower)
                tiles.append(jnp.where(upper_rows, pltpu.roll(odd, 4, 0), even))
                tiles.append(jnp.where(upper_rows, odd, pltpu.roll(even, 4, 0)))
            at = (m // 2) * 8
            side = slice(512 + (at // 256) * 128, 640 + (at // 256) * 128)
            first = at % 256 // 16 * 16
            got = got_ref[first : first + 16, side].astype(F32)
            tiles.append(weight_ref[at : at + 8, :] + got[at % 16 : at % 16 + 8])
            for n in range(5):
                tile = tiles[n].astype(BF16)
                msg_ref[m, :, n * 128 : n * 128 + 128] = tile[0:4]
                msg_ref[m + 1, :, n * 128 : n * 128 + 128] = tile[4:8]


def reduce_kernel(in_ref, bsum_ref, out_ref, rows_ref):
    lower = iota((4, 128), 1) < 64
    weight = [jnp.zeros((4, 128), F32) for core in range(2)]
    left = [jnp.zeros((4, 256), F32) for q in range(16)]

    def spread(parts, owner, row):
        for b in range(2):
            lanes = slice(b * 128, b * 128 + 128)
            near, far = fold(parts[0][:, lanes], parts[1][:, lanes], lower)
            rows_ref[pl.ds(b * 256 + owner * 8 + row, 4, stride=64), :] = near
            rows_ref[pl.ds(512 + b * 256 + owner * 8 + row, 4, stride=64), :] = far

    for r in range(8):
        right = []
        for core in range(2):
            total = jnp.zeros((4, 256), F32)
            for chip in range(8):
                q = chip * 2 + core
                block = in_ref[q * 8 + r].astype(F32)
                total = total + block[:, 0:256]
                left[q] = left[q] + block[:, 256:512]
                weight[core] = weight[core] + block[:, 512:640]
            right.append(total)
        spread(right, r, 4)
    for chip in range(8):
        spread(left[chip * 2 : chip * 2 + 2], chip, 5)
    bias = bsum_ref[...]
    high = bias.astype(BF16).astype(F32)
    tail = [jnp.zeros((2, 128), F32), high, bias - high]
    base = [jnp.concatenate([weight[core]] + tail, 0) for core in range(2)]
    sub = iota((8, 128), 0)
    mine = (sub == 4) | (sub == 5)
    for m in range(128):
        rows = rows_ref[m * 8 : m * 8 + 8, :]
        out_ref[m] = jnp.where(mine, rows, base[(m // 8) % 2]).astype(BF16)


def weight_rows(ref, out_ref):
    upper_rows = iota((8, 128), 0) >= 4
    for p in range(64):
        even, odd = ref[p * 2].astype(F32), ref[p * 2 + 1].astype(F32)
        out_ref[p * 8 : p * 8 + 8, :] = jnp.where(upper_rows, pltpu.roll(odd, 4, 0), even)


def operand_kernel(
    in_ref, update_ref, pair_ref, right_ref, left_ref, bias_ref, rows_ref, plain_ref
):
    for j in range(32):
        at = ((j % 4) * 8 + j // 4) * 16
        plain_ref[pl.ds(j, 16, stride=32), :] = update_ref[at : at + 16, :]
    pair_ref[...] = plain_ref[...].astype(BF16)
    lower = iota((16, 128), 1) < 64
    total = jnp.zeros((8, 128), F32)
    for m in range(128):
        block = in_ref[m].astype(F32)
        rows_ref[m * 8 : m * 8 + 8, :] = block
        total = total + block
    bias_ref[...] = total[6:7] + total[7:8]

    def tiles(row):
        pairs = [
            fold(
                rows_ref[pl.ds(k * 16 + row, 16, stride=64), :],
                rows_ref[pl.ds(k * 16 + 8 + row, 16, stride=64), :],
                lower,
            )
            for k in range(4)
        ]
        return [p[0] for p in pairs], [p[1] for p in pairs]

    for row, out_ref in ((4, right_ref), (5, left_ref)):
        near, far = tiles(row)
        for k, tile in enumerate(near + far):
            for e in range(4):
                out_ref[pl.ds(k * 4 + e, 16, stride=32), :] = tile[:, e * 32 : e * 32 + 32]


def weight_kernel(own_ref, other_ref, out_hbm, rows_ref, sems):
    core = core_index()
    copies = []
    for n, (ref, half) in enumerate(((own_ref, core), (other_ref, 1 - core))):
        weight_rows(ref, rows_ref.at[n])
        at = pl.ds(pl.multiple_of(half * 512, 512), 512)
        copies.append(pltpu.make_async_copy(rows_ref.at[n], out_hbm.at[at], sems.at[n]))
        copies[n].start()
    for copy in copies:
        copy.wait()


def call(kernel, outs, scratch, *args, space=pltpu.VMEM, mib=40, out_space=pltpu.VMEM):
    return pl.pallas_call(
        kernel,
        out_shape=outs,
        in_specs=[pl.BlockSpec(memory_space=space)] * len(args),
        out_specs=tuple([pl.BlockSpec(memory_space=out_space)] * len(outs)),
        scratch_shapes=scratch,
        compiler_params=pltpu.CompilerParams(vmem_limit_bytes=mib * 1024 * 1024),
    )(*args)


def shape(dims, dtype):
    return jax.ShapeDtypeStruct(dims, dtype)


def per_device(left, right, mask, weight, bias, cotangent):
    everyone = [(a, core, b) for a in range(8) for core in range(2) for b in range(8)]

    def place(a, core, b):
        return (a * 2 + core) * 8 + b

    swap = [(place(a, core, b), place(a, 1 - core, b)) for a, core, b in everyone]
    turn = [(place(a, core, b), place(b, core, (a + 4) % 8)) for a, core, b in everyone]
    groups = [[place(a, 0, b) for b in range(8)] for a in range(8)]
    groups += [[place(a, 1, b) for a in range(8)] for b in range(8)]

    def exchange(block, groups=None):
        return lax.all_to_all(block, DEVICES, 0, 0, axis_index_groups=groups, tiled=True)

    left_block, right_block = call(
        prep_kernel,
        (shape((16, 1152), BF16), shape((16, 1152), BF16)),
        [
            pltpu.VMEM((512, 32), BF16),
            pltpu.VMEM((512, 32), BF16),
            pltpu.VMEM((16, 32), jnp.int32),
            pltpu.VMEM((2, 512, 32), F32),
            pltpu.SemaphoreType.DMA((3,)),
        ],
        left.reshape(512, 32),
        right.reshape(512, 32),
        mask,
        space=pltpu.HBM,
        mib=60,
    )
    bias = jnp.broadcast_to(bias, (8, 128))
    left_block, bias = lax.optimization_barrier((lax.ppermute(left_block, DEVICES, turn), bias))
    other_right = lax.ppermute(right_block, DEVICES, swap)
    other_left = lax.ppermute(left_block, DEVICES, swap)
    block = jnp.where(
        core_index() == 0, jnp.stack([left_block, other_left]), jnp.stack([right_block, other_right])
    )
    block = jnp.broadcast_to(block, (8, 2, 16, 1152))
    own = exchange(block, groups).reshape(256, 1152)
    other = lax.ppermute(own, DEVICES, swap)
    lanes = lane_order()

    weight = weight.reshape(1024, 128)
    send, outer, outer_grad, left_all, right_all, mask_i, mask_jd, scaled, inverse, bias_part = call(
        outer_kernel,
        (
            shape((256, 768), BF16),
            shape((512, 1024), BF16),
            shape((512, 1024), BF16),
            shape((256, 512), BF16),
            shape((256, 1024), BF16),
            shape((256, 512), BF16),
            shape((256, 1024), BF16),
            shape((512, 128), BF16),
            shape((512, 128), F32),
            shape((1, 128), F32),
        ),
        [pltpu.VMEM((512, 1024), F32), pltpu.VMEM((512, 1024), F32), pltpu.VMEM((512, 128), F32)],
        own,
        other,
        lanes,
        weight,
        cotangent.reshape(512, 128),
    )
    got = lax.ppermute(send, DEVICES, swap)
    update, right_sum, weight_sum, left_sum = call(
        sums_kernel,
        (shape((512, 128), F32), shape((256, 512), F32), shape((512, 128), F32), shape((256, 512), F32)),
        [],
        outer,
        outer_grad,
        left_all,
        right_all,
        mask_i,
        mask_jd,
        scaled,
        inverse,
        lanes,
        weight,
        bias,
    )
    (parts,) = call(
        pack_kernel,
        (shape((128, 4, 640), BF16),),
        [],
        got,
        right_sum,
        weight_sum,
        left_sum,
    )
    parts = exchange(parts)
    (sums,) = call(
        reduce_kernel, (shape((128, 8, 128), BF16),), [pltpu.VMEM((1024, 128), F32)], parts, bias_part
    )
    sums = exchange(sums)
    other_sums = lax.ppermute(sums, DEVICES, swap)
    pair_update, right_grad, left_grad, bias_grad = call(
        operand_kernel,
        (shape((512, 128), BF16), shape((512, 32), F32), shape((512, 32), F32), shape((1, 128), F32)),
        [pltpu.VMEM((1024, 128), F32), pltpu.VMEM((512, 128), F32)],
        sums,
        update,
    )
    (weight_grad,) = call(
        weight_kernel,
        (shape((1024, 128), F32),),
        [pltpu.VMEM((2, 512, 128), F32), pltpu.SemaphoreType.DMA((2,))],
        sums,
        other_sums,
        out_space=pltpu.HBM,
    )
    return (
        pair_update.reshape(16, 32, 128),
        left_grad.reshape(16, 32, 32),
        right_grad.reshape(16, 32, 32),
        weight_grad.reshape(32, 32, 128),
        bias_grad.reshape(128),
    )


def solution(mesh):
    return jax.shard_map(
        per_device,
        mesh=mesh,
        in_specs=(
            P("seq", "res", None),
            P("seq", "res", None),
            P("seq", "res"),
            P(),
            P(),
            P("seq", "res", None),
        ),
        out_specs=(P("seq", "res", None), P("seq", "res", None), P("seq", "res", None), P(), P()),
        check_vma=False,
    )
```

```python
import jax
import jax.numpy as jnp
import numpy as np
from jax import lax
from jax.experimental import pallas as pl
from jax.experimental.pallas import tpu as pltpu
from jax.sharding import PartitionSpec as P

F32 = jnp.float32
BF16 = jnp.bfloat16
DEVICES = ("seq", "res")
ROWS_ROWS = (((0,), (0,)), ((), ()))
LANES_LANES = (((1,), (1,)), ((), ()))


def iota(shape, dim):
    return lax.broadcasted_iota(jnp.int32, shape, dim)


def swap_groups(blocks):
    lane = iota(blocks[0].shape, 1)
    upper = lane >= 64
    odd = (lane // 32) % 2 == 1
    b0, b1, b2, b3 = blocks
    r0, r1, r2, r3 = (pltpu.roll(b, 64, 1) for b in blocks)
    b0, b2 = jnp.where(upper, r2, b0), jnp.where(upper, b2, r0)
    b1, b3 = jnp.where(upper, r3, b1), jnp.where(upper, b3, r1)
    up1, up3 = pltpu.roll(b1, 32, 1), pltpu.roll(b3, 32, 1)
    down0, down2 = pltpu.roll(b0, 96, 1), pltpu.roll(b2, 96, 1)
    return (
        jnp.where(odd, up1, b0),
        jnp.where(odd, b1, down0),
        jnp.where(odd, up3, b2),
        jnp.where(odd, b3, down2),
    )


def choose(condition):
    return condition.astype(F32).astype(BF16)


def lane_order():
    lane = np.arange(512)
    source = (lane % 16) * 32 + 4 * ((lane % 128) // 16) + lane // 128
    return jnp.asarray(np.arange(512)[:, None] == source[None, :], BF16)


def row_order():
    row = np.arange(256)
    return jnp.asarray((row % 16 * 16 + row // 16)[:, None] == row[None, :], BF16)


def mask_spread():
    lane = np.arange(512)
    pairs = 4 * (lane // 16 % 8) + lane // 128
    lanes = np.concatenate([pairs, np.arange(1024) // 32])
    return jnp.asarray(np.arange(128)[:, None] == lanes[None, :], BF16)


def core_index():
    return lax.axis_index("seq") % 2


def low():
    return iota((8, 128), 1) < 64


def fold(first, second, lower):
    return (
        jnp.where(lower, first, pltpu.roll(second, 64, 1)),
        jnp.where(lower, pltpu.roll(first, 64, 1), second),
    )


def prep_kernel(
    left_hbm, right_hbm, mask_hbm, left_out, right_out, left_ref, right_ref, mask_ref, wide_ref, sems
):
    copies = [
        pltpu.make_async_copy(left_hbm, left_ref, sems.at[0]),
        pltpu.make_async_copy(right_hbm, right_ref, sems.at[1]),
        pltpu.make_async_copy(mask_hbm, mask_ref, sems.at[2]),
    ]
    for copy in copies:
        copy.start()
    for copy in copies:
        copy.wait()
    mask = mask_ref[...].astype(F32).astype(BF16)
    widen = choose(iota((32, 128), 0) == iota((32, 128), 1))
    masks = jnp.dot(mask, widen, preferred_element_type=F32).astype(BF16)
    for n, (ref, out_ref) in enumerate(((left_ref, left_out), (right_ref, right_out))):
        wide_ref[n] = ref[...].astype(F32)
        for k in range(8):
            tile = [wide_ref[n, pl.ds(k * 4 + e, 16, stride=32), :] for e in range(4)]
            out_ref[:, k * 128 : k * 128 + 128] = jnp.concatenate(tile, 1).astype(BF16)
        out_ref[:, 1024:1152] = masks


def cotangent_kernel(cot_ref, rows_ref, bsum_ref, cot32_ref):
    cot32 = cot_ref[...].astype(F32)
    cot32_ref[...] = cot32
    bsum_ref[...] = jnp.sum(cot32, axis=0, keepdims=True)
    for j in range(32):
        at = ((j % 4) * 8 + j // 4) * 16
        rows_ref[at : at + 16, :] = cot32_ref[pl.ds(j, 16, stride=32), :]


def outer_kernel(
    own_ref, other_ref, lanes_ref, spread_ref, w_ref, cot_ref,
    send_ref, x_ref, dy_ref, left_ref, right_ref, mask_i_ref, mask_jd_ref, scaled_ref, inverse_ref,
    y_ref, dx_ref,
):
    core = core_index()
    keep = pl.multiple_of(core * 512, 512)
    give = pl.multiple_of((1 - core) * 512, 512)

    def rows(lanes, of_left):
        return jnp.where(core == (0 if of_left else 1), own_ref[:, lanes], other_ref[:, lanes])

    def turned(block):
        return jnp.concatenate([block[128:256], block[0:128]], 0)

    masks = turned(rows(slice(1024, 1152), True))
    left = turned(rows(pl.ds(keep, 512), True))
    left = jnp.dot(left, lanes_ref[...], preferred_element_type=F32).astype(BF16)
    right = rows(slice(0, 1152), False)
    spread_i = choose(iota((128, 512), 0) == core * 16 + iota((128, 512), 1) % 16)
    masks_j = right[:, 1024:1152]
    mask_i = jnp.dot(masks, spread_i, preferred_element_type=F32)
    mask_j = jnp.dot(masks_j, spread_ref[:, 0:512], preferred_element_type=F32)
    mask_jd = jnp.dot(masks_j, spread_ref[:, 512:1536], preferred_element_type=F32)
    mask_i_ref[...] = mask_i.astype(BF16)
    mask_jd_ref[...] = mask_jd.astype(BF16)
    left = left * mask_i_ref[...]
    right = right[:, 0:1024] * mask_jd_ref[...]
    left_ref[...] = left
    right_ref[...] = right
    both = (mask_i * mask_j).astype(BF16)
    counts = (
        lax.dot_general(both, jnp.ones((256, 128), BF16), ROWS_ROWS, preferred_element_type=F32) + 1e-3
    )
    inverse = 1.0 / counts
    inverse_ref[...] = inverse
    scaled = (cot_ref[...] * inverse).astype(BF16)
    scaled_ref[...] = scaled

    y_ref[...] = lax.dot_general(left, right, ROWS_ROWS, preferred_element_type=F32)
    for u in range(8):
        lanes = slice(u * 128, u * 128 + 128)
        for t in range(8):
            tiles = swap_groups([y_ref[f * 128 + t * 16 : f * 128 + t * 16 + 16, lanes] for f in range(4)])
            for e in range(4):
                at = (e * 8 + u) * 16
                x_ref[at : at + 16, t * 128 : t * 128 + 128] = tiles[e].astype(BF16)

    dx_ref[...] = lax.dot_general(scaled, w_ref[...], LANES_LANES, preferred_element_type=F32)
    for u in range(8):
        lanes = slice(u * 128, u * 128 + 128)
        for t in range(8):
            tiles = swap_groups(
                [dx_ref[(e * 8 + u) * 16 : (e * 8 + u) * 16 + 16, t * 128 : t * 128 + 128] for e in range(4)]
            )
            for f in range(4):
                dy_ref[f * 128 + t * 16 : f * 128 + t * 16 + 16, lanes] = tiles[f].astype(BF16)

    part = right_part(give, left, dy_ref, mask_jd_ref).astype(BF16)
    send_ref[:, 0:512] = part
    part = weight_part(give, x_ref, scaled).astype(BF16)
    send_ref[:, 512:640] = part[0:256]
    send_ref[:, 640:768] = part[256:512]


def right_part(half, left, dy_ref, mask_ref):
    part = jnp.dot(left, dy_ref[:, pl.ds(half, 512)], preferred_element_type=F32)
    return part * mask_ref[:, pl.ds(half, 512)].astype(F32)


def weight_part(half, x_ref, scaled):
    return lax.dot_general(x_ref[:, pl.ds(half, 512)], scaled, ROWS_ROWS, preferred_element_type=F32)


def sums_kernel(
    x_ref, dy_ref, left_in, right_in, mask_i_ref, mask_jd_ref, scaled_ref, inverse_ref, lanes_ref, order_ref, w_ref, bias_ref,
    update_ref, right_ref, weight_ref, left_ref,
):
    keep = pl.multiple_of(core_index() * 512, 512)
    left = lax.dot_general(right_in[...], dy_ref[...], LANES_LANES, preferred_element_type=F32)
    left = (left * mask_i_ref[...].astype(F32)).astype(BF16)
    right_ref[...] = right_part(keep, left_in[...], dy_ref, mask_jd_ref)
    left = lax.dot_general(left, lanes_ref[...], LANES_LANES, preferred_element_type=F32).astype(BF16)
    weight_ref[...] = weight_part(keep, x_ref, scaled_ref[...])
    left_ref[...] = jnp.dot(order_ref[...], left, preferred_element_type=F32)
    update_ref[...] = (
        jnp.dot(x_ref[...], w_ref[...], preferred_element_type=F32) * inverse_ref[...] + bias_ref[0:1, :]
    )


def pack_kernel(got_ref, right_ref, weight_ref, left_ref, order_ref, msg_ref, sum_ref):
    lower = low()
    upper_rows = iota((8, 128), 0) >= 4
    total = (right_ref[...] + got_ref[:, 0:512].astype(F32)).astype(BF16)
    sum_ref[...] = jnp.dot(order_ref[...], total, preferred_element_type=F32)
    for s in range(16):
        for k in range(4):
            m = s * 8 + k * 2
            lanes = slice(k * 128, k * 128 + 128)
            tiles = []
            for ref in (sum_ref, left_ref):
                block = ref[s * 16 : s * 16 + 16, lanes]
                even, odd = fold(block[0:8], block[8:16], lower)
                tiles.append(jnp.where(upper_rows, pltpu.roll(odd, 4, 0), even))
                tiles.append(jnp.where(upper_rows, odd, pltpu.roll(even, 4, 0)))
            at = (m // 2) * 8
            side = slice(512 + (at // 256) * 128, 640 + (at // 256) * 128)
            first = at % 256 // 16 * 16
            got = got_ref[first : first + 16, side].astype(F32)
            tiles.append(weight_ref[at : at + 8, :] + got[at % 16 : at % 16 + 8])
            for n in range(5):
                tile = tiles[n].astype(BF16)
                msg_ref[m, :, n * 128 : n * 128 + 128] = tile[0:4]
                msg_ref[m + 1, :, n * 128 : n * 128 + 128] = tile[4:8]


def reduce_kernel(in_ref, bsum_ref, out_ref, rows_ref):
    lower = iota((4, 128), 1) < 64
    weight = [jnp.zeros((4, 128), F32) for core in range(2)]
    left = [jnp.zeros((4, 256), F32) for q in range(16)]

    def spread(parts, owner, row):
        for b in range(2):
            lanes = slice(b * 128, b * 128 + 128)
            near, far = fold(parts[0][:, lanes], parts[1][:, lanes], lower)
            rows_ref[pl.ds(b * 256 + owner * 8 + row, 4, stride=64), :] = near
            rows_ref[pl.ds(512 + b * 256 + owner * 8 + row, 4, stride=64), :] = far

    for r in range(8):
        right = []
        for core in range(2):
            total = jnp.zeros((4, 256), F32)
            for chip in range(8):
                q = chip * 2 + core
                block = in_ref[q * 8 + r].astype(F32)
                total = total + block[:, 0:256]
                left[q] = left[q] + block[:, 256:512]
                weight[core] = weight[core] + block[:, 512:640]
            right.append(total)
        spread(right, r, 4)
    for chip in range(8):
        spread(left[chip * 2 : chip * 2 + 2], chip, 5)
    bias = bsum_ref[...]
    high = bias.astype(BF16).astype(F32)
    tail = [jnp.zeros((2, 128), F32), high, bias - high]
    base = [jnp.concatenate([weight[core]] + tail, 0) for core in range(2)]
    sub = iota((8, 128), 0)
    mine = (sub == 4) | (sub == 5)
    for m in range(128):
        rows = rows_ref[m * 8 : m * 8 + 8, :]
        out_ref[m] = jnp.where(mine, rows, base[(m // 8) % 2]).astype(BF16)


def weight_rows(ref, out_ref):
    upper_rows = iota((8, 128), 0) >= 4
    for p in range(64):
        even, odd = ref[p * 2].astype(F32), ref[p * 2 + 1].astype(F32)
        out_ref[p * 8 : p * 8 + 8, :] = jnp.where(upper_rows, pltpu.roll(odd, 4, 0), even)


def operand_kernel(
    in_ref, update_ref, pair_ref, right_ref, left_ref, bias_ref, rows_ref, plain_ref
):
    for j in range(32):
        at = ((j % 4) * 8 + j // 4) * 16
        plain_ref[pl.ds(j, 16, stride=32), :] = update_ref[at : at + 16, :]
    pair_ref[...] = plain_ref[...].astype(BF16)
    lower = iota((16, 128), 1) < 64
    total = jnp.zeros((8, 128), F32)
    for m in range(128):
        block = in_ref[m].astype(F32)
        rows_ref[m * 8 : m * 8 + 8, :] = block
        total = total + block
    bias_ref[...] = total[6:7] + total[7:8]

    def tiles(row):
        pairs = [
            fold(
                rows_ref[pl.ds(k * 16 + row, 16, stride=64), :],
                rows_ref[pl.ds(k * 16 + 8 + row, 16, stride=64), :],
                lower,
            )
            for k in range(4)
        ]
        return [p[0] for p in pairs], [p[1] for p in pairs]

    for row, out_ref in ((4, right_ref), (5, left_ref)):
        near, far = tiles(row)
        for k, tile in enumerate(near + far):
            for e in range(4):
                out_ref[pl.ds(k * 4 + e, 16, stride=32), :] = tile[:, e * 32 : e * 32 + 32]


def weight_kernel(own_ref, other_ref, out_hbm, rows_ref, sems):
    core = core_index()
    copies = []
    for n, (ref, half) in enumerate(((own_ref, core), (other_ref, 1 - core))):
        weight_rows(ref, rows_ref.at[n])
        at = pl.ds(pl.multiple_of(half * 512, 512), 512)
        copies.append(pltpu.make_async_copy(rows_ref.at[n], out_hbm.at[at], sems.at[n]))
        copies[n].start()
    for copy in copies:
        copy.wait()


def call(kernel, outs, scratch, *args, space=pltpu.VMEM, mib=40, out_space=pltpu.VMEM):
    return pl.pallas_call(
        kernel,
        out_shape=outs,
        in_specs=[pl.BlockSpec(memory_space=space)] * len(args),
        out_specs=tuple([pl.BlockSpec(memory_space=out_space)] * len(outs)),
        scratch_shapes=scratch,
        compiler_params=pltpu.CompilerParams(vmem_limit_bytes=mib * 1024 * 1024),
    )(*args)


def shape(dims, dtype):
    return jax.ShapeDtypeStruct(dims, dtype)


def per_device(left, right, mask, weight, bias, cotangent):
    everyone = [(a, core, b) for a in range(8) for core in range(2) for b in range(8)]

    def place(a, core, b):
        return (a * 2 + core) * 8 + b

    swap = [(place(a, core, b), place(a, 1 - core, b)) for a, core, b in everyone]
    turn = [(place(a, core, b), place(b, core, (a + 4) % 8)) for a, core, b in everyone]
    groups = [[place(a, 0, b) for b in range(8)] for a in range(8)]
    groups += [[place(a, 1, b) for a in range(8)] for b in range(8)]

    def exchange(block, groups=None):
        return lax.all_to_all(block, DEVICES, 0, 0, axis_index_groups=groups, tiled=True)

    left_block, right_block = call(
        prep_kernel,
        (shape((16, 1152), BF16), shape((16, 1152), BF16)),
        [
            pltpu.VMEM((512, 32), BF16),
            pltpu.VMEM((512, 32), BF16),
            pltpu.VMEM((16, 32), jnp.int32),
            pltpu.VMEM((2, 512, 32), F32),
            pltpu.SemaphoreType.DMA((3,)),
        ],
        left.reshape(512, 32),
        right.reshape(512, 32),
        mask,
        space=pltpu.HBM,
        mib=60,
    )
    bias = jnp.broadcast_to(bias, (8, 128))
    left_block, bias = lax.optimization_barrier((lax.ppermute(left_block, DEVICES, turn), bias))
    other_right = lax.ppermute(right_block, DEVICES, swap)
    other_left = lax.ppermute(left_block, DEVICES, swap)
    block = jnp.where(
        core_index() == 0, jnp.stack([left_block, other_left]), jnp.stack([other_right, right_block])
    )
    block = jnp.broadcast_to(block, (8, 2, 16, 1152))
    own = exchange(block, groups).reshape(256, 1152)
    own, cotangent = lax.optimization_barrier((own, cotangent))
    other = lax.ppermute(own, DEVICES, swap)
    cot_rows, bias_part = call(
        cotangent_kernel,
        (shape((512, 128), F32), shape((1, 128), F32)),
        [pltpu.VMEM((512, 128), F32)],
        cotangent.reshape(512, 128),
    )
    lanes, order = lane_order(), row_order()

    weight = weight.reshape(1024, 128)
    send, outer, outer_grad, left_all, right_all, mask_i, mask_jd, scaled, inverse = call(
        outer_kernel,
        (
            shape((256, 768), BF16),
            shape((512, 1024), BF16),
            shape((512, 1024), BF16),
            shape((256, 512), BF16),
            shape((256, 1024), BF16),
            shape((256, 512), BF16),
            shape((256, 1024), BF16),
            shape((512, 128), BF16),
            shape((512, 128), F32),
        ),
        [pltpu.VMEM((512, 1024), F32), pltpu.VMEM((512, 1024), F32)],
        own,
        other,
        lanes,
        mask_spread(),
        weight,
        cot_rows,
    )
    got = lax.ppermute(send, DEVICES, swap)
    update, right_sum, weight_sum, left_sum = call(
        sums_kernel,
        (shape((512, 128), F32), shape((256, 512), F32), shape((512, 128), F32), shape((256, 512), F32)),
        [],
        outer,
        outer_grad,
        left_all,
        right_all,
        mask_i,
        mask_jd,
        scaled,
        inverse,
        lanes,
        order,
        weight,
        bias,
    )
    (parts,) = call(
        pack_kernel,
        (shape((128, 4, 640), BF16),),
        [pltpu.VMEM((256, 512), F32)],
        got,
        right_sum,
        weight_sum,
        left_sum,
        order,
    )
    parts = exchange(parts)
    (sums,) = call(
        reduce_kernel, (shape((128, 8, 128), BF16),), [pltpu.VMEM((1024, 128), F32)], parts, bias_part
    )
    sums = exchange(sums)
    other_sums = lax.ppermute(sums, DEVICES, swap)
    pair_update, right_grad, left_grad, bias_grad = call(
        operand_kernel,
        (shape((512, 128), BF16), shape((512, 32), F32), shape((512, 32), F32), shape((1, 128), F32)),
        [pltpu.VMEM((1024, 128), F32), pltpu.VMEM((512, 128), F32)],
        sums,
        update,
    )
    (weight_grad,) = call(
        weight_kernel,
        (shape((1024, 128), F32),),
        [pltpu.VMEM((2, 512, 128), F32), pltpu.SemaphoreType.DMA((2,))],
        sums,
        other_sums,
        out_space=pltpu.HBM,
    )
    return (
        pair_update.reshape(16, 32, 128),
        left_grad.reshape(16, 32, 32),
        right_grad.reshape(16, 32, 32),
        weight_grad.reshape(32, 32, 128),
        bias_grad.reshape(128),
    )


def solution(mesh):
    return jax.shard_map(
        per_device,
        mesh=mesh,
        in_specs=(
            P("seq", "res", None),
            P("seq", "res", None),
            P("seq", "res"),
            P(),
            P(),
            P("seq", "res", None),
        ),
        out_specs=(P("seq", "res", None), P("seq", "res", None), P("seq", "res", None), P(), P()),
        check_vma=False,
    )
```

```python
import jax
import jax.numpy as jnp
import numpy as np
from jax import lax
from jax.experimental import pallas as pl
from jax.experimental.pallas import tpu as pltpu
from jax.sharding import PartitionSpec as P

F32 = jnp.float32
BF16 = jnp.bfloat16
DEVICES = ("seq", "res")
ROWS_ROWS = (((0,), (0,)), ((), ()))
LANES_LANES = (((1,), (1,)), ((), ()))


def iota(shape, dim):
    return lax.broadcasted_iota(jnp.int32, shape, dim)


def swap_groups(blocks):
    lane = iota(blocks[0].shape, 1)
    upper = lane >= 64
    odd = (lane // 32) % 2 == 1
    b0, b1, b2, b3 = blocks
    r0, r1, r2, r3 = (pltpu.roll(b, 64, 1) for b in blocks)
    b0, b2 = jnp.where(upper, r2, b0), jnp.where(upper, b2, r0)
    b1, b3 = jnp.where(upper, r3, b1), jnp.where(upper, b3, r1)
    up1, up3 = pltpu.roll(b1, 32, 1), pltpu.roll(b3, 32, 1)
    down0, down2 = pltpu.roll(b0, 96, 1), pltpu.roll(b2, 96, 1)
    return (
        jnp.where(odd, up1, b0),
        jnp.where(odd, b1, down0),
        jnp.where(odd, up3, b2),
        jnp.where(odd, b3, down2),
    )


def choose(condition):
    return condition.astype(F32).astype(BF16)


def lane_order():
    lane = np.arange(512)
    source = (lane % 16) * 32 + 4 * ((lane % 128) // 16) + lane // 128
    return jnp.asarray(np.arange(512)[:, None] == source[None, :], BF16)


def row_order():
    row = np.arange(256)
    return jnp.asarray((row % 16 * 16 + row // 16)[:, None] == row[None, :], BF16)


def mask_spread():
    lane = np.arange(512)
    pairs = 4 * (lane // 16 % 8) + lane // 128
    lanes = np.concatenate([pairs, np.arange(1024) // 32])
    return jnp.asarray(np.arange(128)[:, None] == lanes[None, :], BF16)


def core_index():
    return lax.axis_index("seq") % 2


def low():
    return iota((8, 128), 1) < 64


def fold(first, second, lower):
    return (
        jnp.where(lower, first, pltpu.roll(second, 64, 1)),
        jnp.where(lower, pltpu.roll(first, 64, 1), second),
    )


def prep_kernel(block_hbm, mask_hbm, out_ref, block_ref, mask_ref, wide_ref, sems):
    copies = [pltpu.make_async_copy(mask_hbm, mask_ref, sems.at[4])]
    for n in range(4):
        part = slice(n * 128, n * 128 + 128)
        copies.append(pltpu.make_async_copy(block_hbm.at[part], block_ref.at[part], sems.at[n]))
    for copy in copies:
        copy.start()
    for copy in copies:
        copy.wait()
    wide_ref[...] = block_ref[...].astype(F32)
    for k in range(8):
        tile = [wide_ref[pl.ds(k * 4 + e, 16, stride=32), :] for e in range(4)]
        out_ref[:, k * 128 : k * 128 + 128] = jnp.concatenate(tile, 1).astype(BF16)
    mask = mask_ref[...].astype(F32).astype(BF16)
    widen = choose(iota((32, 128), 0) == iota((32, 128), 1))
    out_ref[:, 1024:1152] = jnp.dot(mask, widen, preferred_element_type=F32).astype(BF16)


def cotangent_kernel(cot_ref, rows_ref, bsum_ref, cot32_ref):
    cot32 = cot_ref[...].astype(F32)
    cot32_ref[...] = cot32
    bsum_ref[...] = jnp.sum(cot32, axis=0, keepdims=True)
    for j in range(32):
        at = ((j % 4) * 8 + j // 4) * 16
        rows_ref[at : at + 16, :] = cot32_ref[pl.ds(j, 16, stride=32), :]


def outer_kernel(
    own_ref, other_ref, lanes_ref, spread_ref, w_ref, cot_ref,
    send_ref, x_ref, dy_ref, left_ref, right_ref, mask_i_ref, mask_jd_ref, scaled_ref, inverse_ref,
    y_ref, dx_ref,
):
    core = core_index()
    keep = pl.multiple_of(core * 512, 512)
    give = pl.multiple_of((1 - core) * 512, 512)

    def rows(lanes, of_left):
        return jnp.where(core == (0 if of_left else 1), own_ref[:, lanes], other_ref[:, lanes])

    def turned(block):
        return jnp.concatenate([block[128:256], block[0:128]], 0)

    masks = turned(rows(slice(1024, 1152), True))
    left = turned(rows(pl.ds(keep, 512), True))
    left = jnp.dot(left, lanes_ref[...], preferred_element_type=F32).astype(BF16)
    right = rows(slice(0, 1152), False)
    spread_i = choose(iota((128, 512), 0) == core * 16 + iota((128, 512), 1) % 16)
    masks_j = right[:, 1024:1152]
    mask_i = jnp.dot(masks, spread_i, preferred_element_type=F32)
    mask_j = jnp.dot(masks_j, spread_ref[:, 0:512], preferred_element_type=F32)
    mask_jd = jnp.dot(masks_j, spread_ref[:, 512:1536], preferred_element_type=F32)
    mask_i_ref[...] = mask_i.astype(BF16)
    mask_jd_ref[...] = mask_jd.astype(BF16)
    left = left * mask_i_ref[...]
    right = right[:, 0:1024] * mask_jd_ref[...]
    left_ref[...] = left
    right_ref[...] = right
    both = (mask_i * mask_j).astype(BF16)
    counts = (
        lax.dot_general(both, jnp.ones((256, 128), BF16), ROWS_ROWS, preferred_element_type=F32) + 1e-3
    )
    inverse = 1.0 / counts
    inverse_ref[...] = inverse
    scaled = (cot_ref[...] * inverse).astype(BF16)
    scaled_ref[...] = scaled

    y_ref[...] = lax.dot_general(left, right, ROWS_ROWS, preferred_element_type=F32)
    for u in range(8):
        lanes = slice(u * 128, u * 128 + 128)
        for t in range(8):
            tiles = swap_groups([y_ref[f * 128 + t * 16 : f * 128 + t * 16 + 16, lanes] for f in range(4)])
            for e in range(4):
                at = (e * 8 + u) * 16
                x_ref[at : at + 16, t * 128 : t * 128 + 128] = tiles[e].astype(BF16)

    dx_ref[...] = lax.dot_general(scaled, w_ref[...], LANES_LANES, preferred_element_type=F32)
    for u in range(8):
        lanes = slice(u * 128, u * 128 + 128)
        for t in range(8):
            tiles = swap_groups(
                [dx_ref[(e * 8 + u) * 16 : (e * 8 + u) * 16 + 16, t * 128 : t * 128 + 128] for e in range(4)]
            )
            for f in range(4):
                dy_ref[f * 128 + t * 16 : f * 128 + t * 16 + 16, lanes] = tiles[f].astype(BF16)

    part = right_part(give, left, dy_ref, mask_jd_ref).astype(BF16)
    send_ref[:, 0:512] = part
    part = weight_part(give, x_ref, scaled).astype(BF16)
    send_ref[:, 512:640] = part[0:256]
    send_ref[:, 640:768] = part[256:512]


def right_part(half, left, dy_ref, mask_ref):
    part = jnp.dot(left, dy_ref[:, pl.ds(half, 512)], preferred_element_type=F32)
    return part * mask_ref[:, pl.ds(half, 512)].astype(F32)


def weight_part(half, x_ref, scaled):
    return lax.dot_general(x_ref[:, pl.ds(half, 512)], scaled, ROWS_ROWS, preferred_element_type=F32)


def sums_kernel(
    x_ref, dy_ref, left_in, right_in, mask_i_ref, mask_jd_ref, scaled_ref, inverse_ref, lanes_ref, order_ref, w_ref, bias_ref,
    update_ref, right_ref, weight_ref, left_ref,
):
    keep = pl.multiple_of(core_index() * 512, 512)
    left = lax.dot_general(right_in[...], dy_ref[...], LANES_LANES, preferred_element_type=F32)
    left = (left * mask_i_ref[...].astype(F32)).astype(BF16)
    right_ref[...] = right_part(keep, left_in[...], dy_ref, mask_jd_ref)
    left = lax.dot_general(left, lanes_ref[...], LANES_LANES, preferred_element_type=F32).astype(BF16)
    weight_ref[...] = weight_part(keep, x_ref, scaled_ref[...])
    left_ref[...] = jnp.dot(order_ref[...], left, preferred_element_type=F32)
    update_ref[...] = (
        jnp.dot(x_ref[...], w_ref[...], preferred_element_type=F32) * inverse_ref[...] + bias_ref[0:1, :]
    )


def pack_kernel(got_ref, right_ref, weight_ref, left_ref, order_ref, msg_ref, sum_ref):
    lower = low()
    upper_rows = iota((8, 128), 0) >= 4
    total = (right_ref[...] + got_ref[:, 0:512].astype(F32)).astype(BF16)
    sum_ref[...] = jnp.dot(order_ref[...], total, preferred_element_type=F32)
    for s in range(16):
        for k in range(4):
            m = s * 8 + k * 2
            lanes = slice(k * 128, k * 128 + 128)
            tiles = []
            for ref in (sum_ref, left_ref):
                block = ref[s * 16 : s * 16 + 16, lanes]
                even, odd = fold(block[0:8], block[8:16], lower)
                tiles.append(jnp.where(upper_rows, pltpu.roll(odd, 4, 0), even))
                tiles.append(jnp.where(upper_rows, odd, pltpu.roll(even, 4, 0)))
            at = (m // 2) * 8
            side = slice(512 + (at // 256) * 128, 640 + (at // 256) * 128)
            first = at % 256 // 16 * 16
            got = got_ref[first : first + 16, side].astype(F32)
            tiles.append(weight_ref[at : at + 8, :] + got[at % 16 : at % 16 + 8])
            for n in range(5):
                tile = tiles[n].astype(BF16)
                msg_ref[m, :, n * 128 : n * 128 + 128] = tile[0:4]
                msg_ref[m + 1, :, n * 128 : n * 128 + 128] = tile[4:8]


def reduce_kernel(in_ref, bsum_ref, out_ref, rows_ref):
    lower = iota((4, 128), 1) < 64
    weight = [jnp.zeros((4, 128), F32) for core in range(2)]
    left = [jnp.zeros((4, 256), F32) for q in range(16)]

    def spread(parts, owner, row):
        for b in range(2):
            lanes = slice(b * 128, b * 128 + 128)
            near, far = fold(parts[0][:, lanes], parts[1][:, lanes], lower)
            rows_ref[pl.ds(b * 256 + owner * 8 + row, 4, stride=64), :] = near
            rows_ref[pl.ds(512 + b * 256 + owner * 8 + row, 4, stride=64), :] = far

    for r in range(8):
        right = []
        for core in range(2):
            total = jnp.zeros((4, 256), F32)
            for chip in range(8):
                q = chip * 2 + core
                block = in_ref[q * 8 + r].astype(F32)
                total = total + block[:, 0:256]
                left[q] = left[q] + block[:, 256:512]
                weight[core] = weight[core] + block[:, 512:640]
            right.append(total)
        spread(right, r, 4)
    for chip in range(8):
        spread(left[chip * 2 : chip * 2 + 2], chip, 5)
    bias = bsum_ref[...]
    high = bias.astype(BF16).astype(F32)
    tail = [jnp.zeros((2, 128), F32), high, bias - high]
    base = [jnp.concatenate([weight[core]] + tail, 0) for core in range(2)]
    sub = iota((8, 128), 0)
    mine = (sub == 4) | (sub == 5)
    for m in range(128):
        rows = rows_ref[m * 8 : m * 8 + 8, :]
        out_ref[m] = jnp.where(mine, rows, base[(m // 8) % 2]).astype(BF16)


def weight_rows(ref, out_ref):
    upper_rows = iota((8, 128), 0) >= 4
    for p in range(64):
        even, odd = ref[p * 2].astype(F32), ref[p * 2 + 1].astype(F32)
        out_ref[p * 8 : p * 8 + 8, :] = jnp.where(upper_rows, pltpu.roll(odd, 4, 0), even)


def operand_kernel(
    in_ref, update_ref, pair_ref, right_ref, left_ref, bias_ref, rows_ref, plain_ref
):
    for j in range(32):
        at = ((j % 4) * 8 + j // 4) * 16
        plain_ref[pl.ds(j, 16, stride=32), :] = update_ref[at : at + 16, :]
    pair_ref[...] = plain_ref[...].astype(BF16)
    lower = iota((16, 128), 1) < 64
    total = jnp.zeros((8, 128), F32)
    for m in range(128):
        block = in_ref[m].astype(F32)
        rows_ref[m * 8 : m * 8 + 8, :] = block
        total = total + block
    bias_ref[...] = total[6:7] + total[7:8]

    def tiles(row):
        pairs = [
            fold(
                rows_ref[pl.ds(k * 16 + row, 16, stride=64), :],
                rows_ref[pl.ds(k * 16 + 8 + row, 16, stride=64), :],
                lower,
            )
            for k in range(4)
        ]
        return [p[0] for p in pairs], [p[1] for p in pairs]

    for row, out_ref in ((4, right_ref), (5, left_ref)):
        near, far = tiles(row)
        for k, tile in enumerate(near + far):
            for e in range(4):
                out_ref[pl.ds(k * 4 + e, 16, stride=32), :] = tile[:, e * 32 : e * 32 + 32]


def weight_kernel(own_ref, other_ref, out_hbm, rows_ref, sems):
    core = core_index()
    copies = []
    for n, (ref, half) in enumerate(((own_ref, core), (other_ref, 1 - core))):
        weight_rows(ref, rows_ref.at[n])
        at = pl.ds(pl.multiple_of(half * 512, 512), 512)
        copies.append(pltpu.make_async_copy(rows_ref.at[n], out_hbm.at[at], sems.at[n]))
        copies[n].start()
    for copy in copies:
        copy.wait()


def call(kernel, outs, scratch, *args, space=pltpu.VMEM, mib=40, out_space=pltpu.VMEM):
    return pl.pallas_call(
        kernel,
        out_shape=outs,
        in_specs=[pl.BlockSpec(memory_space=space)] * len(args),
        out_specs=tuple([pl.BlockSpec(memory_space=out_space)] * len(outs)),
        scratch_shapes=scratch,
        compiler_params=pltpu.CompilerParams(vmem_limit_bytes=mib * 1024 * 1024),
    )(*args)


def shape(dims, dtype):
    return jax.ShapeDtypeStruct(dims, dtype)


def per_device(left, right, mask, weight, bias, cotangent):
    everyone = [(a, core, b) for a in range(8) for core in range(2) for b in range(8)]

    def place(a, core, b):
        return (a * 2 + core) * 8 + b

    swap = [(place(a, core, b), place(a, 1 - core, b)) for a, core, b in everyone]
    turn = [(place(a, core, b), place(b, core, (a + 4) % 8)) for a, core, b in everyone]
    groups = [[place(a, 0, b) for b in range(8)] for a in range(8)]
    groups += [[place(a, 1, b) for a in range(8)] for b in range(8)]

    def exchange(block, groups=None):
        return lax.all_to_all(block, DEVICES, 0, 0, axis_index_groups=groups, tiled=True)

    def prepared(block):
        (block,) = call(
            prep_kernel,
            (shape((16, 1152), BF16),),
            [
                pltpu.VMEM((512, 32), BF16),
                pltpu.VMEM((16, 32), jnp.int32),
                pltpu.VMEM((512, 32), F32),
                pltpu.SemaphoreType.DMA((5,)),
            ],
            block.reshape(512, 32),
            mask,
            space=pltpu.HBM,
            mib=60,
        )
        return block

    left_block, right_block = prepared(left), prepared(right)
    bias = jnp.broadcast_to(bias, (8, 128))
    left_block, bias = lax.optimization_barrier((lax.ppermute(left_block, DEVICES, turn), bias))
    other_right = lax.ppermute(right_block, DEVICES, swap)
    other_left = lax.ppermute(left_block, DEVICES, swap)
    block = jnp.where(
        core_index() == 0, jnp.stack([left_block, other_left]), jnp.stack([other_right, right_block])
    )
    block = jnp.broadcast_to(block, (8, 2, 16, 1152))
    own = exchange(block, groups).reshape(256, 1152)
    own, cotangent = lax.optimization_barrier((own, cotangent))
    other = lax.ppermute(own, DEVICES, swap)
    cot_rows, bias_part = call(
        cotangent_kernel,
        (shape((512, 128), F32), shape((1, 128), F32)),
        [pltpu.VMEM((512, 128), F32)],
        cotangent.reshape(512, 128),
    )
    lanes, order = lane_order(), row_order()

    weight = weight.reshape(1024, 128)
    send, outer, outer_grad, left_all, right_all, mask_i, mask_jd, scaled, inverse = call(
        outer_kernel,
        (
            shape((256, 768), BF16),
            shape((512, 1024), BF16),
            shape((512, 1024), BF16),
            shape((256, 512), BF16),
            shape((256, 1024), BF16),
            shape((256, 512), BF16),
            shape((256, 1024), BF16),
            shape((512, 128), BF16),
            shape((512, 128), F32),
        ),
        [pltpu.VMEM((512, 1024), F32), pltpu.VMEM((512, 1024), F32)],
        own,
        other,
        lanes,
        mask_spread(),
        weight,
        cot_rows,
    )
    got = lax.ppermute(send, DEVICES, swap)
    update, right_sum, weight_sum, left_sum = call(
        sums_kernel,
        (shape((512, 128), F32), shape((256, 512), F32), shape((512, 128), F32), shape((256, 512), F32)),
        [],
        outer,
        outer_grad,
        left_all,
        right_all,
        mask_i,
        mask_jd,
        scaled,
        inverse,
        lanes,
        order,
        weight,
        bias,
    )
    (parts,) = call(
        pack_kernel,
        (shape((128, 4, 640), BF16),),
        [pltpu.VMEM((256, 512), F32)],
        got,
        right_sum,
        weight_sum,
        left_sum,
        order,
    )
    parts = exchange(parts)
    (sums,) = call(
        reduce_kernel, (shape((128, 8, 128), BF16),), [pltpu.VMEM((1024, 128), F32)], parts, bias_part
    )
    sums = exchange(sums)
    other_sums = lax.ppermute(sums, DEVICES, swap)
    pair_update, right_grad, left_grad, bias_grad = call(
        operand_kernel,
        (shape((512, 128), BF16), shape((512, 32), F32), shape((512, 32), F32), shape((1, 128), F32)),
        [pltpu.VMEM((1024, 128), F32), pltpu.VMEM((512, 128), F32)],
        sums,
        update,
    )
    (weight_grad,) = call(
        weight_kernel,
        (shape((1024, 128), F32),),
        [pltpu.VMEM((2, 512, 128), F32), pltpu.SemaphoreType.DMA((2,))],
        sums,
        other_sums,
        out_space=pltpu.HBM,
    )
    return (
        pair_update.reshape(16, 32, 128),
        left_grad.reshape(16, 32, 32),
        right_grad.reshape(16, 32, 32),
        weight_grad.reshape(32, 32, 128),
        bias_grad.reshape(128),
    )


def solution(mesh):
    return jax.shard_map(
        per_device,
        mesh=mesh,
        in_specs=(
            P("seq", "res", None),
            P("seq", "res", None),
            P("seq", "res"),
            P(),
            P(),
            P("seq", "res", None),
        ),
        out_specs=(P("seq", "res", None), P("seq", "res", None), P("seq", "res", None), P(), P()),
        check_vma=False,
    )
```

```python
import jax
import jax.numpy as jnp
import numpy as np
from jax import lax
from jax.experimental import pallas as pl
from jax.experimental.pallas import tpu as pltpu
from jax.sharding import PartitionSpec as P

F32 = jnp.float32
BF16 = jnp.bfloat16
DEVICES = ("seq", "res")
ROWS_ROWS = (((0,), (0,)), ((), ()))
LANES_LANES = (((1,), (1,)), ((), ()))


def iota(shape, dim):
    return lax.broadcasted_iota(jnp.int32, shape, dim)


def swap_groups(blocks):
    lane = iota(blocks[0].shape, 1)
    upper = lane >= 64
    odd = (lane // 32) % 2 == 1
    b0, b1, b2, b3 = blocks
    r0, r1, r2, r3 = (pltpu.roll(b, 64, 1) for b in blocks)
    b0, b2 = jnp.where(upper, r2, b0), jnp.where(upper, b2, r0)
    b1, b3 = jnp.where(upper, r3, b1), jnp.where(upper, b3, r1)
    up1, up3 = pltpu.roll(b1, 32, 1), pltpu.roll(b3, 32, 1)
    down0, down2 = pltpu.roll(b0, 96, 1), pltpu.roll(b2, 96, 1)
    return (
        jnp.where(odd, up1, b0),
        jnp.where(odd, b1, down0),
        jnp.where(odd, up3, b2),
        jnp.where(odd, b3, down2),
    )


def choose(condition):
    return condition.astype(F32).astype(BF16)


def lane_order():
    lane = np.arange(512)
    source = (lane % 16) * 32 + 4 * ((lane % 128) // 16) + lane // 128
    return jnp.asarray(np.arange(512)[:, None] == source[None, :], BF16)


def row_order():
    row = np.arange(256)
    source = row % 2 * 128 + row % 16 // 2 * 16 + row // 16
    return jnp.asarray(source[:, None] == row[None, :], BF16)


def mask_spread():
    lane = np.arange(512)
    pairs = 4 * (lane // 16 % 8) + lane // 128
    lanes = np.concatenate([pairs, np.arange(1024) // 32])
    source = np.arange(128)[None, :, None] - 32 * np.arange(2)[:, None, None]
    return jnp.asarray(source == lanes[None, None, :], BF16)


def core_index():
    return lax.axis_index("seq") % 2


def low():
    return iota((8, 128), 1) < 64


def fold(first, second, lower):
    return (
        jnp.where(lower, first, pltpu.roll(second, 64, 1)),
        jnp.where(lower, pltpu.roll(first, 64, 1), second),
    )


def prep_kernel(block_hbm, mask_hbm, out_ref, block_ref, mask_ref, wide_ref, sems):
    copies = [pltpu.make_async_copy(mask_hbm, mask_ref, sems.at[4])]
    for n in range(4):
        part = slice(n * 128, n * 128 + 128)
        copies.append(pltpu.make_async_copy(block_hbm.at[part], block_ref.at[part], sems.at[n]))
    for copy in copies:
        copy.start()
    for copy in copies:
        copy.wait()
    wide_ref[...] = block_ref[...].astype(F32)
    for k in range(8):
        tile = [wide_ref[pl.ds(k * 4 + e, 16, stride=32), :] for e in range(4)]
        out_ref[:, k * 128 : k * 128 + 128] = jnp.concatenate(tile, 1).astype(BF16)
    mask = mask_ref[...].astype(F32).astype(BF16)
    widen = choose(iota((32, 128), 0) + 32 * core_index() == iota((32, 128), 1))
    out_ref[:, 1024:1152] = jnp.dot(mask, widen, preferred_element_type=F32).astype(BF16)


def cotangent_kernel(cot_ref, rows_ref, bsum_ref, cot32_ref):
    cot32 = cot_ref[...].astype(F32)
    cot32_ref[...] = cot32
    bsum_ref[...] = jnp.sum(cot32, axis=0, keepdims=True)
    for j in range(32):
        at = ((j % 4) * 8 + j // 4) * 16
        rows_ref[at : at + 16, :] = cot32_ref[pl.ds(j, 16, stride=32), :]


def outer_kernel(
    own_ref, other_ref, lanes_ref, spread_ref, w_ref, cot_ref,
    send_ref, x_ref, dy_ref, left_ref, right_ref, mask_i_ref, mask_jd_ref, scaled_ref, inverse_ref,
    y_ref, dx_ref,
):
    core = core_index()
    keep = pl.multiple_of(core * 512, 512)
    give = pl.multiple_of((1 - core) * 512, 512)

    def rows(lanes, of_left):
        return jnp.where(core == (0 if of_left else 1), own_ref[:, lanes], other_ref[:, lanes])

    def turned(block):
        return jnp.concatenate([block[64:128], block[0:64]], 0)

    left = jnp.concatenate([turned(rows(pl.ds(n * 1024 + keep, 512), True)) for n in range(2)], 0)
    left = jnp.dot(left, lanes_ref[...], preferred_element_type=F32).astype(BF16)
    right = jnp.concatenate([rows(slice(n * 1024, n * 1024 + 1024), False) for n in range(2)], 0)
    masks, masks_j = turned(rows(slice(2048, 2176), True)), rows(slice(2048, 2176), False)
    lane = iota((128, 512), 1) % 16 + core * 16

    def spread(block, tables):
        return jnp.concatenate([jnp.dot(block, table, preferred_element_type=F32) for table in tables], 0)

    mask_i = spread(masks, [choose(iota((128, 512), 0) == lane + 32 * n) for n in range(2)])
    mask_j = spread(masks_j, [spread_ref[n, :, 0:512] for n in range(2)])
    mask_jd = spread(masks_j, [spread_ref[n, :, 512:1536] for n in range(2)])
    mask_i_ref[...] = mask_i.astype(BF16)
    mask_jd_ref[...] = mask_jd.astype(BF16)
    left = left * mask_i_ref[...]
    right = right * mask_jd_ref[...]
    left_ref[...] = left
    right_ref[...] = right
    both = (mask_i * mask_j).astype(BF16)
    counts = (
        lax.dot_general(both, jnp.ones((256, 128), BF16), ROWS_ROWS, preferred_element_type=F32) + 1e-3
    )
    inverse = 1.0 / counts
    inverse_ref[...] = inverse
    scaled = (cot_ref[...] * inverse).astype(BF16)
    scaled_ref[...] = scaled

    y_ref[...] = lax.dot_general(left, right, ROWS_ROWS, preferred_element_type=F32)
    for u in range(8):
        lanes = slice(u * 128, u * 128 + 128)
        for t in range(8):
            tiles = swap_groups([y_ref[f * 128 + t * 16 : f * 128 + t * 16 + 16, lanes] for f in range(4)])
            for e in range(4):
                at = (e * 8 + u) * 16
                x_ref[at : at + 16, t * 128 : t * 128 + 128] = tiles[e].astype(BF16)

    dx_ref[...] = lax.dot_general(scaled, w_ref[...], LANES_LANES, preferred_element_type=F32)
    for u in range(8):
        lanes = slice(u * 128, u * 128 + 128)
        for t in range(8):
            tiles = swap_groups(
                [dx_ref[(e * 8 + u) * 16 : (e * 8 + u) * 16 + 16, t * 128 : t * 128 + 128] for e in range(4)]
            )
            for f in range(4):
                dy_ref[f * 128 + t * 16 : f * 128 + t * 16 + 16, lanes] = tiles[f].astype(BF16)

    part = right_part(give, left, dy_ref, mask_jd_ref).astype(BF16)
    send_ref[:, 0:512] = part
    part = weight_part(give, x_ref, scaled).astype(BF16)
    send_ref[:, 512:640] = part[0:256]
    send_ref[:, 640:768] = part[256:512]


def right_part(half, left, dy_ref, mask_ref):
    part = jnp.dot(left, dy_ref[:, pl.ds(half, 512)], preferred_element_type=F32)
    return part * mask_ref[:, pl.ds(half, 512)].astype(F32)


def weight_part(half, x_ref, scaled):
    return lax.dot_general(x_ref[:, pl.ds(half, 512)], scaled, ROWS_ROWS, preferred_element_type=F32)


def sums_kernel(
    x_ref, dy_ref, left_in, right_in, mask_i_ref, mask_jd_ref, scaled_ref, inverse_ref, lanes_ref, order_ref, w_ref, bias_ref,
    update_ref, right_ref, weight_ref, left_ref,
):
    keep = pl.multiple_of(core_index() * 512, 512)
    left = lax.dot_general(right_in[...], dy_ref[...], LANES_LANES, preferred_element_type=F32)
    left = (left * mask_i_ref[...].astype(F32)).astype(BF16)
    right_ref[...] = right_part(keep, left_in[...], dy_ref, mask_jd_ref)
    left = lax.dot_general(left, lanes_ref[...], LANES_LANES, preferred_element_type=F32).astype(BF16)
    weight_ref[...] = weight_part(keep, x_ref, scaled_ref[...])
    left_ref[...] = jnp.dot(order_ref[...], left, preferred_element_type=F32)
    update_ref[...] = (
        jnp.dot(x_ref[...], w_ref[...], preferred_element_type=F32) * inverse_ref[...] + bias_ref[0:1, :]
    )


def pack_kernel(got_ref, right_ref, weight_ref, left_ref, order_ref, msg_ref, sum_ref):
    lower = low()
    upper_rows = iota((8, 128), 0) >= 4
    total = (right_ref[...] + got_ref[:, 0:512].astype(F32)).astype(BF16)
    sum_ref[...] = jnp.dot(order_ref[...], total, preferred_element_type=F32)
    for s in range(16):
        for k in range(4):
            m = s * 8 + k * 2
            lanes = slice(k * 128, k * 128 + 128)
            tiles = []
            for ref in (sum_ref, left_ref):
                block = ref[s * 16 : s * 16 + 16, lanes]
                even, odd = fold(block[0:8], block[8:16], lower)
                tiles.append(jnp.where(upper_rows, pltpu.roll(odd, 4, 0), even))
                tiles.append(jnp.where(upper_rows, odd, pltpu.roll(even, 4, 0)))
            at = (m // 2) * 8
            side = slice(512 + (at // 256) * 128, 640 + (at // 256) * 128)
            first = at % 256 // 16 * 16
            got = got_ref[first : first + 16, side].astype(F32)
            tiles.append(weight_ref[at : at + 8, :] + got[at % 16 : at % 16 + 8])
            for n in range(5):
                tile = tiles[n].astype(BF16)
                msg_ref[m, :, n * 128 : n * 128 + 128] = tile[0:4]
                msg_ref[m + 1, :, n * 128 : n * 128 + 128] = tile[4:8]


def reduce_kernel(in_ref, bsum_ref, out_ref, rows_ref):
    lower = iota((4, 128), 1) < 64
    weight = [jnp.zeros((4, 128), F32) for core in range(2)]
    left = [jnp.zeros((4, 256), F32) for q in range(16)]

    def spread(parts, owner, row):
        for b in range(2):
            lanes = slice(b * 128, b * 128 + 128)
            near, far = fold(parts[0][:, lanes], parts[1][:, lanes], lower)
            rows_ref[pl.ds(b * 256 + owner * 8 + row, 4, stride=64), :] = near
            rows_ref[pl.ds(512 + b * 256 + owner * 8 + row, 4, stride=64), :] = far

    for r in range(8):
        right = []
        for core in range(2):
            total = jnp.zeros((4, 256), F32)
            for chip in range(8):
                q = chip * 2 + core
                block = in_ref[q * 8 + r].astype(F32)
                total = total + block[:, 0:256]
                left[q] = left[q] + block[:, 256:512]
                weight[core] = weight[core] + block[:, 512:640]
            right.append(total)
        spread(right, r, 4)
    for chip in range(8):
        spread(left[chip * 2 : chip * 2 + 2], chip, 5)
    bias = bsum_ref[...]
    high = bias.astype(BF16).astype(F32)
    tail = [jnp.zeros((2, 128), F32), high, bias - high]
    base = [jnp.concatenate([weight[core]] + tail, 0) for core in range(2)]
    sub = iota((8, 128), 0)
    mine = (sub == 4) | (sub == 5)
    for m in range(128):
        rows = rows_ref[m * 8 : m * 8 + 8, :]
        out_ref[m] = jnp.where(mine, rows, base[(m // 8) % 2]).astype(BF16)


def weight_rows(ref, out_ref):
    upper_rows = iota((8, 128), 0) >= 4
    for p in range(64):
        even, odd = ref[p * 2].astype(F32), ref[p * 2 + 1].astype(F32)
        out_ref[p * 8 : p * 8 + 8, :] = jnp.where(upper_rows, pltpu.roll(odd, 4, 0), even)


def operand_kernel(
    in_ref, update_ref, pair_ref, right_ref, left_ref, bias_ref, rows_ref, plain_ref
):
    for j in range(32):
        at = ((j % 4) * 8 + j // 4) * 16
        plain_ref[pl.ds(j, 16, stride=32), :] = update_ref[at : at + 16, :]
    pair_ref[...] = plain_ref[...].astype(BF16)
    lower = iota((16, 128), 1) < 64
    total = jnp.zeros((8, 128), F32)
    for m in range(128):
        block = in_ref[m].astype(F32)
        rows_ref[m * 8 : m * 8 + 8, :] = block
        total = total + block
    bias_ref[...] = total[6:7] + total[7:8]

    def tiles(row):
        pairs = [
            fold(
                rows_ref[pl.ds(k * 16 + row, 16, stride=64), :],
                rows_ref[pl.ds(k * 16 + 8 + row, 16, stride=64), :],
                lower,
            )
            for k in range(4)
        ]
        return [p[0] for p in pairs], [p[1] for p in pairs]

    for row, out_ref in ((4, right_ref), (5, left_ref)):
        near, far = tiles(row)
        for k, tile in enumerate(near + far):
            for e in range(4):
                out_ref[pl.ds(k * 4 + e, 16, stride=32), :] = tile[:, e * 32 : e * 32 + 32]


def weight_kernel(own_ref, other_ref, out_hbm, rows_ref, sems):
    core = core_index()
    copies = []
    for n, (ref, half) in enumerate(((own_ref, core), (other_ref, 1 - core))):
        weight_rows(ref, rows_ref.at[n])
        at = pl.ds(pl.multiple_of(half * 512, 512), 512)
        copies.append(pltpu.make_async_copy(rows_ref.at[n], out_hbm.at[at], sems.at[n]))
        copies[n].start()
    for copy in copies:
        copy.wait()


def call(kernel, outs, scratch, *args, space=pltpu.VMEM, mib=40, out_space=pltpu.VMEM):
    return pl.pallas_call(
        kernel,
        out_shape=outs,
        in_specs=[pl.BlockSpec(memory_space=space)] * len(args),
        out_specs=tuple([pl.BlockSpec(memory_space=out_space)] * len(outs)),
        scratch_shapes=scratch,
        compiler_params=pltpu.CompilerParams(vmem_limit_bytes=mib * 1024 * 1024),
    )(*args)


def shape(dims, dtype):
    return jax.ShapeDtypeStruct(dims, dtype)


def per_device(left, right, mask, weight, bias, cotangent):
    everyone = [(a, core, b) for a in range(8) for core in range(2) for b in range(8)]

    def place(a, core, b):
        return (a * 2 + core) * 8 + b

    swap = [(place(a, core, b), place(a, 1 - core, b)) for a, core, b in everyone]
    turn = [(place(a, core, b), place(b, core, (a + 4) % 8)) for a, core, b in everyone]
    groups = [[place(a, 0, b) for b in range(8)] for a in range(8)]
    groups += [[place(a, 1, b) for a in range(8)] for b in range(8)]

    def exchange(block, groups=None):
        return lax.all_to_all(block, DEVICES, 0, 0, axis_index_groups=groups, tiled=True)

    def prepared(block):
        (block,) = call(
            prep_kernel,
            (shape((16, 1152), BF16),),
            [
                pltpu.VMEM((512, 32), BF16),
                pltpu.VMEM((16, 32), jnp.int32),
                pltpu.VMEM((512, 32), F32),
                pltpu.SemaphoreType.DMA((5,)),
            ],
            block.reshape(512, 32),
            mask,
            space=pltpu.HBM,
            mib=60,
        )
        return block

    left_block, right_block = prepared(left), prepared(right)
    bias = jnp.broadcast_to(bias, (8, 128))
    left_block, bias = lax.optimization_barrier((lax.ppermute(left_block, DEVICES, turn), bias))
    other_right = lax.ppermute(right_block, DEVICES, swap)
    other_left = lax.ppermute(left_block, DEVICES, swap)
    first = core_index() == 0
    near = jnp.where(first, left_block, other_right)
    far = jnp.where(first, other_left, right_block)
    block = jnp.concatenate([near[:, :1024], far[:, :1024], near[:, 1024:] + far[:, 1024:]], 1)
    own = exchange(jnp.broadcast_to(block, (8, 16, 2176)), groups).reshape(128, 2176)
    own, cotangent = lax.optimization_barrier((own, cotangent))
    other = lax.ppermute(own, DEVICES, swap)
    cot_rows, bias_part = call(
        cotangent_kernel,
        (shape((512, 128), F32), shape((1, 128), F32)),
        [pltpu.VMEM((512, 128), F32)],
        cotangent.reshape(512, 128),
    )
    lanes, order = lane_order(), row_order()

    weight = weight.reshape(1024, 128)
    send, outer, outer_grad, left_all, right_all, mask_i, mask_jd, scaled, inverse = call(
        outer_kernel,
        (
            shape((256, 768), BF16),
            shape((512, 1024), BF16),
            shape((512, 1024), BF16),
            shape((256, 512), BF16),
            shape((256, 1024), BF16),
            shape((256, 512), BF16),
            shape((256, 1024), BF16),
            shape((512, 128), BF16),
            shape((512, 128), F32),
        ),
        [pltpu.VMEM((512, 1024), F32), pltpu.VMEM((512, 1024), F32)],
        own,
        other,
        lanes,
        mask_spread(),
        weight,
        cot_rows,
    )
    got = lax.ppermute(send, DEVICES, swap)
    update, right_sum, weight_sum, left_sum = call(
        sums_kernel,
        (shape((512, 128), F32), shape((256, 512), F32), shape((512, 128), F32), shape((256, 512), F32)),
        [],
        outer,
        outer_grad,
        left_all,
        right_all,
        mask_i,
        mask_jd,
        scaled,
        inverse,
        lanes,
        order,
        weight,
        bias,
    )
    (parts,) = call(
        pack_kernel,
        (shape((128, 4, 640), BF16),),
        [pltpu.VMEM((256, 512), F32)],
        got,
        right_sum,
        weight_sum,
        left_sum,
        order,
    )
    parts = exchange(parts)
    (sums,) = call(
        reduce_kernel, (shape((128, 8, 128), BF16),), [pltpu.VMEM((1024, 128), F32)], parts, bias_part
    )
    sums = exchange(sums)
    other_sums = lax.ppermute(sums, DEVICES, swap)
    pair_update, right_grad, left_grad, bias_grad = call(
        operand_kernel,
        (shape((512, 128), BF16), shape((512, 32), F32), shape((512, 32), F32), shape((1, 128), F32)),
        [pltpu.VMEM((1024, 128), F32), pltpu.VMEM((512, 128), F32)],
        sums,
        update,
    )
    (weight_grad,) = call(
        weight_kernel,
        (shape((1024, 128), F32),),
        [pltpu.VMEM((2, 512, 128), F32), pltpu.SemaphoreType.DMA((2,))],
        sums,
        other_sums,
        out_space=pltpu.HBM,
    )
    return (
        pair_update.reshape(16, 32, 128),
        left_grad.reshape(16, 32, 32),
        right_grad.reshape(16, 32, 32),
        weight_grad.reshape(32, 32, 128),
        bias_grad.reshape(128),
    )


def solution(mesh):
    return jax.shard_map(
        per_device,
        mesh=mesh,
        in_specs=(
            P("seq", "res", None),
            P("seq", "res", None),
            P("seq", "res"),
            P(),
            P(),
            P("seq", "res", None),
        ),
        out_specs=(P("seq", "res", None), P("seq", "res", None), P("seq", "res", None), P(), P()),
        check_vma=False,
    )
```

```python
import jax
import jax.numpy as jnp
import numpy as np
from jax import lax
from jax.experimental import pallas as pl
from jax.experimental.pallas import tpu as pltpu
from jax.sharding import PartitionSpec as P

F32 = jnp.float32
BF16 = jnp.bfloat16
DEVICES = ("seq", "res")
ROWS_ROWS = (((0,), (0,)), ((), ()))
LANES_LANES = (((1,), (1,)), ((), ()))


def iota(shape, dim):
    return lax.broadcasted_iota(jnp.int32, shape, dim)


def swap_groups(blocks):
    lane = iota(blocks[0].shape, 1)
    upper = lane >= 64
    odd = (lane // 32) % 2 == 1
    b0, b1, b2, b3 = blocks
    r0, r1, r2, r3 = (pltpu.roll(b, 64, 1) for b in blocks)
    b0, b2 = jnp.where(upper, r2, b0), jnp.where(upper, b2, r0)
    b1, b3 = jnp.where(upper, r3, b1), jnp.where(upper, b3, r1)
    up1, up3 = pltpu.roll(b1, 32, 1), pltpu.roll(b3, 32, 1)
    down0, down2 = pltpu.roll(b0, 96, 1), pltpu.roll(b2, 96, 1)
    return (
        jnp.where(odd, up1, b0),
        jnp.where(odd, b1, down0),
        jnp.where(odd, up3, b2),
        jnp.where(odd, b3, down2),
    )


def choose(condition):
    return condition.astype(F32).astype(BF16)


def lane_order():
    lane = np.arange(512)
    source = (lane % 16) * 32 + 4 * ((lane % 128) // 16) + lane // 128
    return jnp.asarray(np.arange(512)[:, None] == source[None, :], BF16)


def row_order():
    row = np.arange(256)
    source = row % 2 * 128 + row % 16 // 2 * 16 + row // 16
    return jnp.asarray(source[:, None] == row[None, :], BF16)


def mask_spread():
    lane = np.arange(512)
    pairs = 4 * (lane // 16 % 8) + lane // 128
    lanes = np.concatenate([pairs, np.arange(1024) // 32])
    source = np.arange(128)[None, :, None] - 32 * np.arange(2)[:, None, None]
    return jnp.asarray(source == lanes[None, None, :], BF16)


def core_index():
    return lax.axis_index("seq") % 2


def low():
    return iota((8, 128), 1) < 64


def fold(first, second, lower):
    return (
        jnp.where(lower, first, pltpu.roll(second, 64, 1)),
        jnp.where(lower, pltpu.roll(first, 64, 1), second),
    )


def prep_kernel(block_hbm, mask_hbm, out_ref, block_ref, mask_ref, wide_ref, sems):
    copies = [pltpu.make_async_copy(mask_hbm, mask_ref, sems.at[4])]
    for n in range(4):
        part = slice(n * 128, n * 128 + 128)
        copies.append(pltpu.make_async_copy(block_hbm.at[part], block_ref.at[part], sems.at[n]))
    for copy in copies:
        copy.start()
    for copy in copies:
        copy.wait()
    wide_ref[...] = block_ref[...].astype(F32)
    for k in range(8):
        tile = [wide_ref[pl.ds(k * 4 + e, 16, stride=32), :] for e in range(4)]
        out_ref[:, k * 128 : k * 128 + 128] = jnp.concatenate(tile, 1).astype(BF16)
    mask = mask_ref[...].astype(F32).astype(BF16)
    widen = choose(iota((32, 128), 0) + 32 * core_index() == iota((32, 128), 1))
    out_ref[:, 1024:1152] = jnp.dot(mask, widen, preferred_element_type=F32).astype(BF16)


def cotangent_kernel(cot_ref, rows_ref, bsum_ref, cot32_ref):
    cot32 = cot_ref[...].astype(F32)
    cot32_ref[...] = cot32
    bsum_ref[...] = jnp.sum(cot32, axis=0, keepdims=True)
    for j in range(32):
        at = ((j % 4) * 8 + j // 4) * 16
        rows_ref[at : at + 16, :] = cot32_ref[pl.ds(j, 16, stride=32), :]


def outer_kernel(
    own_ref, other_ref, lanes_ref, spread_ref, w_ref, cot_ref,
    send_ref, x_ref, dy_ref, left_ref, right_ref, mask_i_ref, mask_jd_ref, scaled_ref, inverse_ref,
    y_ref, dx_ref,
):
    core = core_index()
    keep = pl.multiple_of(core * 512, 512)
    give = pl.multiple_of((1 - core) * 512, 512)

    def rows(lanes, of_left):
        return jnp.where(core == (0 if of_left else 1), own_ref[:, lanes], other_ref[:, lanes])

    def turned(block):
        return jnp.concatenate([block[64:128], block[0:64]], 0)

    left = jnp.concatenate([turned(rows(pl.ds(n * 1024 + keep, 512), True)) for n in range(2)], 0)
    left = jnp.dot(left, lanes_ref[...], preferred_element_type=F32).astype(BF16)
    right = jnp.concatenate([rows(slice(n * 1024, n * 1024 + 1024), False) for n in range(2)], 0)
    masks, masks_j = turned(rows(slice(2048, 2176), True)), rows(slice(2048, 2176), False)
    lane = iota((128, 512), 1) % 16 + core * 16

    def spread(block, tables):
        return jnp.concatenate([jnp.dot(block, table, preferred_element_type=F32) for table in tables], 0)

    mask_i = spread(masks, [choose(iota((128, 512), 0) == lane + 32 * n) for n in range(2)])
    mask_j = spread(masks_j, [spread_ref[n, :, 0:512] for n in range(2)])
    mask_jd = spread(masks_j, [spread_ref[n, :, 512:1536] for n in range(2)])
    mask_i_ref[...] = mask_i.astype(BF16)
    mask_jd_ref[...] = mask_jd.astype(BF16)
    left = left * mask_i_ref[...]
    right = right * mask_jd_ref[...]
    left_ref[...] = left
    right_ref[...] = right
    both = (mask_i * mask_j).astype(BF16)
    counts = (
        lax.dot_general(both, jnp.ones((256, 128), BF16), ROWS_ROWS, preferred_element_type=F32) + 1e-3
    )
    inverse = 1.0 / counts
    inverse_ref[...] = inverse
    scaled = (cot_ref[...] * inverse).astype(BF16)
    scaled_ref[...] = scaled

    dx_ref[...] = lax.dot_general(scaled, w_ref[...], LANES_LANES, preferred_element_type=F32)
    y_ref[...] = lax.dot_general(left, right, ROWS_ROWS, preferred_element_type=F32)
    for u in range(8):
        lanes = slice(u * 128, u * 128 + 128)
        for t in range(8):
            tiles = swap_groups([y_ref[f * 128 + t * 16 : f * 128 + t * 16 + 16, lanes] for f in range(4)])
            for e in range(4):
                at = (e * 8 + u) * 16
                x_ref[at : at + 16, t * 128 : t * 128 + 128] = tiles[e].astype(BF16)

    part = weight_part(give, x_ref, scaled).astype(BF16)
    send_ref[:, 512:640] = part[0:256]
    send_ref[:, 640:768] = part[256:512]

    for u in range(8):
        lanes = slice(u * 128, u * 128 + 128)
        for t in range(8):
            tiles = swap_groups(
                [dx_ref[(e * 8 + u) * 16 : (e * 8 + u) * 16 + 16, t * 128 : t * 128 + 128] for e in range(4)]
            )
            for f in range(4):
                dy_ref[f * 128 + t * 16 : f * 128 + t * 16 + 16, lanes] = tiles[f].astype(BF16)

    part = right_part(give, left, dy_ref, mask_jd_ref).astype(BF16)
    send_ref[:, 0:512] = part


def right_part(half, left, dy_ref, mask_ref):
    part = jnp.dot(left, dy_ref[:, pl.ds(half, 512)], preferred_element_type=F32)
    return part * mask_ref[:, pl.ds(half, 512)].astype(F32)


def weight_part(half, x_ref, scaled):
    return lax.dot_general(x_ref[:, pl.ds(half, 512)], scaled, ROWS_ROWS, preferred_element_type=F32)


def sums_kernel(
    x_ref, dy_ref, left_in, right_in, mask_i_ref, mask_jd_ref, scaled_ref, inverse_ref, lanes_ref, order_ref, w_ref, bias_ref,
    update_ref, right_ref, weight_ref, left_ref,
):
    keep = pl.multiple_of(core_index() * 512, 512)
    left = lax.dot_general(right_in[...], dy_ref[...], LANES_LANES, preferred_element_type=F32)
    left = (left * mask_i_ref[...].astype(F32)).astype(BF16)
    right_ref[...] = right_part(keep, left_in[...], dy_ref, mask_jd_ref)
    left = lax.dot_general(left, lanes_ref[...], LANES_LANES, preferred_element_type=F32).astype(BF16)
    weight_ref[...] = weight_part(keep, x_ref, scaled_ref[...])
    left_ref[...] = jnp.dot(order_ref[...], left, preferred_element_type=F32)
    update_ref[...] = (
        jnp.dot(x_ref[...], w_ref[...], preferred_element_type=F32) * inverse_ref[...] + bias_ref[0:1, :]
    )


def pack_kernel(got_ref, right_ref, weight_ref, left_ref, order_ref, msg_ref, sum_ref):
    lower = low()
    upper_rows = iota((8, 128), 0) >= 4
    total = (right_ref[...] + got_ref[:, 0:512].astype(F32)).astype(BF16)
    sum_ref[...] = jnp.dot(order_ref[...], total, preferred_element_type=F32)
    for s in range(16):
        for k in range(4):
            m = s * 8 + k * 2
            lanes = slice(k * 128, k * 128 + 128)
            tiles = []
            for ref in (sum_ref, left_ref):
                block = ref[s * 16 : s * 16 + 16, lanes]
                even, odd = fold(block[0:8], block[8:16], lower)
                tiles.append(jnp.where(upper_rows, pltpu.roll(odd, 4, 0), even))
                tiles.append(jnp.where(upper_rows, odd, pltpu.roll(even, 4, 0)))
            at = (m // 2) * 8
            side = slice(512 + (at // 256) * 128, 640 + (at // 256) * 128)
            first = at % 256 // 16 * 16
            got = got_ref[first : first + 16, side].astype(F32)
            tiles.append(weight_ref[at : at + 8, :] + got[at % 16 : at % 16 + 8])
            for n in range(5):
                tile = tiles[n].astype(BF16)
                msg_ref[m, :, n * 128 : n * 128 + 128] = tile[0:4]
                msg_ref[m + 1, :, n * 128 : n * 128 + 128] = tile[4:8]


def reduce_kernel(in_ref, bsum_ref, out_ref, rows_ref):
    lower = iota((4, 128), 1) < 64
    weight = [jnp.zeros((4, 128), F32) for core in range(2)]
    left = [jnp.zeros((4, 256), F32) for q in range(16)]

    def spread(parts, owner, row):
        for b in range(2):
            lanes = slice(b * 128, b * 128 + 128)
            near, far = fold(parts[0][:, lanes], parts[1][:, lanes], lower)
            rows_ref[pl.ds(b * 256 + owner * 8 + row, 4, stride=64), :] = near
            rows_ref[pl.ds(512 + b * 256 + owner * 8 + row, 4, stride=64), :] = far

    for r in range(8):
        right = []
        for core in range(2):
            total = jnp.zeros((4, 256), F32)
            for chip in range(8):
                q = chip * 2 + core
                block = in_ref[q * 8 + r].astype(F32)
                total = total + block[:, 0:256]
                left[q] = left[q] + block[:, 256:512]
                weight[core] = weight[core] + block[:, 512:640]
            right.append(total)
        spread(right, r, 4)
    for chip in range(8):
        spread(left[chip * 2 : chip * 2 + 2], chip, 5)
    bias = bsum_ref[...]
    high = bias.astype(BF16).astype(F32)
    tail = [jnp.zeros((2, 128), F32), high, bias - high]
    base = [jnp.concatenate([weight[core]] + tail, 0) for core in range(2)]
    sub = iota((8, 128), 0)
    mine = (sub == 4) | (sub == 5)
    for m in range(128):
        rows = rows_ref[m * 8 : m * 8 + 8, :]
        out_ref[m] = jnp.where(mine, rows, base[(m // 8) % 2]).astype(BF16)


def weight_rows(ref, out_ref, side):
    upper_rows = iota((8, 128), 0) >= 4
    for p in range(side * 32, side * 32 + 32):
        even, odd = ref[p * 2].astype(F32), ref[p * 2 + 1].astype(F32)
        out_ref[p * 8 : p * 8 + 8, :] = jnp.where(upper_rows, pltpu.roll(odd, 4, 0), even)


def operand_kernel(
    in_ref, update_ref, pair_ref, right_ref, left_ref, bias_ref, rows_ref, plain_ref
):
    for j in range(32):
        at = ((j % 4) * 8 + j // 4) * 16
        plain_ref[pl.ds(j, 16, stride=32), :] = update_ref[at : at + 16, :]
    pair_ref[...] = plain_ref[...].astype(BF16)
    lower = iota((16, 128), 1) < 64
    total = jnp.zeros((8, 128), F32)
    for m in range(128):
        block = in_ref[m].astype(F32)
        rows_ref[m * 8 : m * 8 + 8, :] = block
        total = total + block
    bias_ref[...] = total[6:7] + total[7:8]

    def tiles(row):
        pairs = [
            fold(
                rows_ref[pl.ds(k * 16 + row, 16, stride=64), :],
                rows_ref[pl.ds(k * 16 + 8 + row, 16, stride=64), :],
                lower,
            )
            for k in range(4)
        ]
        return [p[0] for p in pairs], [p[1] for p in pairs]

    for row, out_ref in ((4, right_ref), (5, left_ref)):
        near, far = tiles(row)
        for k, tile in enumerate(near + far):
            for e in range(4):
                out_ref[pl.ds(k * 4 + e, 16, stride=32), :] = tile[:, e * 32 : e * 32 + 32]


def weight_kernel(own_ref, other_ref, out_hbm, rows_ref, sems):
    core = core_index()
    copies = []
    for n, (ref, half) in enumerate(((own_ref, core), (other_ref, 1 - core))):
        for side in range(2):
            weight_rows(ref, rows_ref.at[n], side)
            at = pl.ds(pl.multiple_of(half * 512 + side * 256, 256), 256)
            part = rows_ref.at[n, side * 256 : side * 256 + 256]
            copies.append(pltpu.make_async_copy(part, out_hbm.at[at], sems.at[n * 2 + side]))
            copies[-1].start()
    for copy in copies:
        copy.wait()


def call(kernel, outs, scratch, *args, space=pltpu.VMEM, mib=40, out_space=pltpu.VMEM):
    return pl.pallas_call(
        kernel,
        out_shape=outs,
        in_specs=[pl.BlockSpec(memory_space=space)] * len(args),
        out_specs=tuple([pl.BlockSpec(memory_space=out_space)] * len(outs)),
        scratch_shapes=scratch,
        compiler_params=pltpu.CompilerParams(vmem_limit_bytes=mib * 1024 * 1024),
    )(*args)


def shape(dims, dtype):
    return jax.ShapeDtypeStruct(dims, dtype)


def per_device(left, right, mask, weight, bias, cotangent):
    everyone = [(a, core, b) for a in range(8) for core in range(2) for b in range(8)]

    def place(a, core, b):
        return (a * 2 + core) * 8 + b

    swap = [(place(a, core, b), place(a, 1 - core, b)) for a, core, b in everyone]
    turn = [(place(a, core, b), place(b, core, (a + 4) % 8)) for a, core, b in everyone]
    groups = [[place(a, 0, b) for b in range(8)] for a in range(8)]
    groups += [[place(a, 1, b) for a in range(8)] for b in range(8)]

    def exchange(block, groups=None):
        return lax.all_to_all(block, DEVICES, 0, 0, axis_index_groups=groups, tiled=True)

    def prepared(block):
        (block,) = call(
            prep_kernel,
            (shape((16, 1152), BF16),),
            [
                pltpu.VMEM((512, 32), BF16),
                pltpu.VMEM((16, 32), jnp.int32),
                pltpu.VMEM((512, 32), F32),
                pltpu.SemaphoreType.DMA((5,)),
            ],
            block.reshape(512, 32),
            mask,
            space=pltpu.HBM,
            mib=60,
        )
        return block

    left_block, right_block = prepared(left), prepared(right)
    bias = jnp.broadcast_to(bias, (8, 128))
    left_block, bias = lax.optimization_barrier((lax.ppermute(left_block, DEVICES, turn), bias))
    other_right = lax.ppermute(right_block, DEVICES, swap)
    other_left = lax.ppermute(left_block, DEVICES, swap)
    first = core_index() == 0
    near = jnp.where(first, left_block, other_right)
    far = jnp.where(first, other_left, right_block)
    block = jnp.concatenate([near[:, :1024], far[:, :1024], near[:, 1024:] + far[:, 1024:]], 1)
    own = exchange(jnp.broadcast_to(block, (8, 16, 2176)), groups).reshape(128, 2176)
    own, cotangent = lax.optimization_barrier((own, cotangent))
    other = lax.ppermute(own, DEVICES, swap)
    cot_rows, bias_part = call(
        cotangent_kernel,
        (shape((512, 128), F32), shape((1, 128), F32)),
        [pltpu.VMEM((512, 128), F32)],
        cotangent.reshape(512, 128),
    )
    lanes, order = lane_order(), row_order()

    weight = weight.reshape(1024, 128)
    send, outer, outer_grad, left_all, right_all, mask_i, mask_jd, scaled, inverse = call(
        outer_kernel,
        (
            shape((256, 768), BF16),
            shape((512, 1024), BF16),
            shape((512, 1024), BF16),
            shape((256, 512), BF16),
            shape((256, 1024), BF16),
            shape((256, 512), BF16),
            shape((256, 1024), BF16),
            shape((512, 128), BF16),
            shape((512, 128), F32),
        ),
        [pltpu.VMEM((512, 1024), F32), pltpu.VMEM((512, 1024), F32)],
        own,
        other,
        lanes,
        mask_spread(),
        weight,
        cot_rows,
    )
    got = lax.ppermute(send, DEVICES, swap)
    update, right_sum, weight_sum, left_sum = call(
        sums_kernel,
        (shape((512, 128), F32), shape((256, 512), F32), shape((512, 128), F32), shape((256, 512), F32)),
        [],
        outer,
        outer_grad,
        left_all,
        right_all,
        mask_i,
        mask_jd,
        scaled,
        inverse,
        lanes,
        order,
        weight,
        bias,
    )
    (parts,) = call(
        pack_kernel,
        (shape((128, 4, 640), BF16),),
        [pltpu.VMEM((256, 512), F32)],
        got,
        right_sum,
        weight_sum,
        left_sum,
        order,
    )
    parts = exchange(parts)
    (sums,) = call(
        reduce_kernel, (shape((128, 8, 128), BF16),), [pltpu.VMEM((1024, 128), F32)], parts, bias_part
    )
    sums = exchange(sums)
    other_sums = lax.ppermute(sums, DEVICES, swap)
    pair_update, right_grad, left_grad, bias_grad = call(
        operand_kernel,
        (shape((512, 128), BF16), shape((512, 32), F32), shape((512, 32), F32), shape((1, 128), F32)),
        [pltpu.VMEM((1024, 128), F32), pltpu.VMEM((512, 128), F32)],
        sums,
        update,
    )
    (weight_grad,) = call(
        weight_kernel,
        (shape((1024, 128), F32),),
        [pltpu.VMEM((2, 512, 128), F32), pltpu.SemaphoreType.DMA((4,))],
        sums,
        other_sums,
        out_space=pltpu.HBM,
    )
    return (
        pair_update.reshape(16, 32, 128),
        left_grad.reshape(16, 32, 32),
        right_grad.reshape(16, 32, 32),
        weight_grad.reshape(32, 32, 128),
        bias_grad.reshape(128),
    )


def solution(mesh):
    return jax.shard_map(
        per_device,
        mesh=mesh,
        in_specs=(
            P("seq", "res", None),
            P("seq", "res", None),
            P("seq", "res"),
            P(),
            P(),
            P("seq", "res", None),
        ),
        out_specs=(P("seq", "res", None), P("seq", "res", None), P("seq", "res", None), P(), P()),
        check_vma=False,
    )
```

```python
import jax
import jax.numpy as jnp
import numpy as np
from jax import lax
from jax.experimental import pallas as pl
from jax.experimental.pallas import tpu as pltpu
from jax.sharding import PartitionSpec as P

F32 = jnp.float32
BF16 = jnp.bfloat16
DEVICES = ("seq", "res")
ROWS_ROWS = (((0,), (0,)), ((), ()))
LANES_LANES = (((1,), (1,)), ((), ()))


def iota(shape, dim):
    return lax.broadcasted_iota(jnp.int32, shape, dim)


def swap_groups(blocks):
    lane = iota(blocks[0].shape, 1)
    upper = lane >= 64
    odd = (lane // 32) % 2 == 1
    b0, b1, b2, b3 = blocks
    r0, r1, r2, r3 = (pltpu.roll(b, 64, 1) for b in blocks)
    b0, b2 = jnp.where(upper, r2, b0), jnp.where(upper, b2, r0)
    b1, b3 = jnp.where(upper, r3, b1), jnp.where(upper, b3, r1)
    up1, up3 = pltpu.roll(b1, 32, 1), pltpu.roll(b3, 32, 1)
    down0, down2 = pltpu.roll(b0, 96, 1), pltpu.roll(b2, 96, 1)
    return (
        jnp.where(odd, up1, b0),
        jnp.where(odd, b1, down0),
        jnp.where(odd, up3, b2),
        jnp.where(odd, b3, down2),
    )


def choose(condition):
    return condition.astype(F32).astype(BF16)


def lane_order():
    lane = np.arange(512)
    source = (lane % 16) * 32 + 4 * ((lane % 128) // 16) + lane // 128
    return jnp.asarray(np.arange(512)[:, None] == source[None, :], BF16)


def row_order():
    row = np.arange(256)
    source = row % 2 * 128 + row % 16 // 2 * 16 + row // 16
    return jnp.asarray(source[:, None] == row[None, :], BF16)


def mask_spread():
    lane = np.arange(512)
    pairs = 4 * (lane // 16 % 8) + lane // 128
    lanes = np.concatenate([pairs, np.arange(1024) // 32])
    source = np.arange(128)[None, :, None] - 32 * np.arange(2)[:, None, None]
    return jnp.asarray(source == lanes[None, None, :], BF16)


def core_index():
    return lax.axis_index("seq") % 2


def low():
    return iota((8, 128), 1) < 64


def fold(first, second, lower):
    return (
        jnp.where(lower, first, pltpu.roll(second, 64, 1)),
        jnp.where(lower, pltpu.roll(first, 64, 1), second),
    )


def prep_kernel(block_hbm, mask_hbm, out_ref, block_ref, mask_ref, wide_ref, sems):
    copies = [pltpu.make_async_copy(mask_hbm, mask_ref, sems.at[4])]
    for n in range(4):
        part = slice(n * 128, n * 128 + 128)
        copies.append(pltpu.make_async_copy(block_hbm.at[part], block_ref.at[part], sems.at[n]))
    for copy in copies:
        copy.start()
    for copy in copies:
        copy.wait()
    wide_ref[...] = block_ref[...].astype(F32)
    for k in range(8):
        tile = [wide_ref[pl.ds(k * 4 + e, 16, stride=32), :] for e in range(4)]
        out_ref[:, k * 128 : k * 128 + 128] = jnp.concatenate(tile, 1).astype(BF16)
    mask = mask_ref[...].astype(F32).astype(BF16)
    widen = choose(iota((32, 128), 0) + 32 * core_index() == iota((32, 128), 1))
    out_ref[:, 1024:1152] = jnp.dot(mask, widen, preferred_element_type=F32).astype(BF16)


def cotangent_kernel(cot_ref, rows_ref, bsum_ref, cot32_ref):
    cot32 = cot_ref[...].astype(F32)
    cot32_ref[...] = cot32
    bsum_ref[...] = jnp.sum(cot32, axis=0, keepdims=True)
    for j in range(32):
        at = ((j % 4) * 8 + j // 4) * 16
        rows_ref[at : at + 16, :] = cot32_ref[pl.ds(j, 16, stride=32), :]


def outer_kernel(
    own_ref, other_ref, lanes_ref, spread_ref, w_ref, cot_ref,
    send_ref, x_ref, dy_ref, left_ref, right_ref, mask_i_ref, mask_jd_ref, scaled_ref, inverse_ref,
    y_ref, dx_ref,
):
    core = core_index()
    keep = pl.multiple_of(core * 512, 512)
    give = pl.multiple_of((1 - core) * 512, 512)

    def rows(lanes, of_left):
        return jnp.where(core == (0 if of_left else 1), own_ref[:, lanes], other_ref[:, lanes])

    def turned(block):
        return jnp.concatenate([block[64:128], block[0:64]], 0)

    left = jnp.concatenate([turned(rows(pl.ds(n * 1024 + keep, 512), True)) for n in range(2)], 0)
    left = jnp.dot(left, lanes_ref[...], preferred_element_type=F32).astype(BF16)
    right = jnp.concatenate([rows(slice(n * 1024, n * 1024 + 1024), False) for n in range(2)], 0)
    masks, masks_j = turned(rows(slice(2048, 2176), True)), rows(slice(2048, 2176), False)
    lane = iota((128, 512), 1) % 16 + core * 16

    def spread(block, tables):
        return jnp.concatenate([jnp.dot(block, table, preferred_element_type=F32) for table in tables], 0)

    mask_i = spread(masks, [choose(iota((128, 512), 0) == lane + 32 * n) for n in range(2)])
    mask_j = spread(masks_j, [spread_ref[n, :, 0:512] for n in range(2)])
    mask_jd = spread(masks_j, [spread_ref[n, :, 512:1536] for n in range(2)])
    mask_i_ref[...] = mask_i.astype(BF16)
    mask_jd_ref[...] = mask_jd.astype(BF16)
    left = left * mask_i_ref[...]
    right = right * mask_jd_ref[...]
    left_ref[...] = left
    right_ref[...] = right
    both = (mask_i * mask_j).astype(BF16)
    counts = (
        lax.dot_general(both, jnp.ones((256, 128), BF16), ROWS_ROWS, preferred_element_type=F32) + 1e-3
    )
    inverse = 1.0 / counts
    inverse_ref[...] = inverse
    scaled = (cot_ref[...] * inverse).astype(BF16)
    scaled_ref[...] = scaled

    dx_ref[...] = lax.dot_general(scaled, w_ref[...], LANES_LANES, preferred_element_type=F32)
    y_ref[...] = lax.dot_general(left, right, ROWS_ROWS, preferred_element_type=F32)
    for u in range(8):
        lanes = slice(u * 128, u * 128 + 128)
        for t in range(8):
            tiles = swap_groups([y_ref[f * 128 + t * 16 : f * 128 + t * 16 + 16, lanes] for f in range(4)])
            for e in range(4):
                at = (e * 8 + u) * 16
                x_ref[at : at + 16, t * 128 : t * 128 + 128] = tiles[e].astype(BF16)

    part = weight_part(give, x_ref, scaled).astype(BF16)
    send_ref[:, 512:640] = part[0:256]
    send_ref[:, 640:768] = part[256:512]

    for u in range(8):
        lanes = slice(u * 128, u * 128 + 128)
        for t in range(8):
            tiles = swap_groups(
                [dx_ref[(e * 8 + u) * 16 : (e * 8 + u) * 16 + 16, t * 128 : t * 128 + 128] for e in range(4)]
            )
            for f in range(4):
                dy_ref[f * 128 + t * 16 : f * 128 + t * 16 + 16, lanes] = tiles[f].astype(BF16)

    part = right_part(give, left, dy_ref, mask_jd_ref).astype(BF16)
    send_ref[:, 0:512] = part


def right_part(half, left, dy_ref, mask_ref):
    part = jnp.dot(left, dy_ref[:, pl.ds(half, 512)], preferred_element_type=F32)
    return part * mask_ref[:, pl.ds(half, 512)].astype(F32)


def weight_part(half, x_ref, scaled):
    return lax.dot_general(x_ref[:, pl.ds(half, 512)], scaled, ROWS_ROWS, preferred_element_type=F32)


def sums_kernel(
    x_ref, dy_ref, left_in, right_in, mask_i_ref, mask_jd_ref, scaled_ref, inverse_ref, lanes_ref, order_ref, w_ref, bias_ref,
    update_ref, right_ref, weight_ref, left_ref,
):
    keep = pl.multiple_of(core_index() * 512, 512)
    left = lax.dot_general(right_in[...], dy_ref[...], LANES_LANES, preferred_element_type=F32)
    left = (left * mask_i_ref[...].astype(F32)).astype(BF16)
    right_ref[...] = right_part(keep, left_in[...], dy_ref, mask_jd_ref)
    left = lax.dot_general(left, lanes_ref[...], LANES_LANES, preferred_element_type=F32).astype(BF16)
    weight_ref[...] = weight_part(keep, x_ref, scaled_ref[...])
    left_ref[...] = jnp.dot(order_ref[...], left, preferred_element_type=F32)
    update_ref[...] = (
        jnp.dot(x_ref[...], w_ref[...], preferred_element_type=F32) * inverse_ref[...] + bias_ref[0:1, :]
    )


def pack_kernel(got_ref, right_ref, weight_ref, left_ref, order_ref, msg_ref, sum_ref):
    lower = low()
    upper_rows = iota((8, 128), 0) >= 4
    for k in range(4):
        lanes = slice(k * 128, k * 128 + 128)
        total = (right_ref[:, lanes] + got_ref[:, lanes].astype(F32)).astype(BF16)
        sum_ref[:, lanes] = jnp.dot(order_ref[...], total, preferred_element_type=F32)
        for s in range(16):
            m = s * 8 + k * 2
            tiles = []
            for ref in (sum_ref, left_ref):
                block = ref[s * 16 : s * 16 + 16, lanes]
                even, odd = fold(block[0:8], block[8:16], lower)
                tiles.append(jnp.where(upper_rows, pltpu.roll(odd, 4, 0), even))
                tiles.append(jnp.where(upper_rows, odd, pltpu.roll(even, 4, 0)))
            at = (m // 2) * 8
            side = slice(512 + (at // 256) * 128, 640 + (at // 256) * 128)
            first = at % 256 // 16 * 16
            got = got_ref[first : first + 16, side].astype(F32)
            tiles.append(weight_ref[at : at + 8, :] + got[at % 16 : at % 16 + 8])
            for n in range(5):
                tile = tiles[n].astype(BF16)
                msg_ref[m, :, n * 128 : n * 128 + 128] = tile[0:4]
                msg_ref[m + 1, :, n * 128 : n * 128 + 128] = tile[4:8]


def reduce_kernel(in_ref, bsum_ref, out_ref, rows_ref):
    lower = iota((4, 128), 1) < 64
    weight = [jnp.zeros((4, 128), F32) for core in range(2)]
    left = [jnp.zeros((4, 256), F32) for q in range(16)]

    def spread(parts, owner, row):
        for b in range(2):
            lanes = slice(b * 128, b * 128 + 128)
            near, far = fold(parts[0][:, lanes], parts[1][:, lanes], lower)
            rows_ref[pl.ds(b * 256 + owner * 8 + row, 4, stride=64), :] = near
            rows_ref[pl.ds(512 + b * 256 + owner * 8 + row, 4, stride=64), :] = far

    for r in range(8):
        right = []
        for core in range(2):
            total = jnp.zeros((4, 256), F32)
            for chip in range(8):
                q = chip * 2 + core
                block = in_ref[q * 8 + r].astype(F32)
                total = total + block[:, 0:256]
                left[q] = left[q] + block[:, 256:512]
                weight[core] = weight[core] + block[:, 512:640]
            right.append(total)
        spread(right, r, 4)
    for chip in range(8):
        spread(left[chip * 2 : chip * 2 + 2], chip, 5)
    bias = bsum_ref[...]
    high = bias.astype(BF16).astype(F32)
    tail = [jnp.zeros((2, 128), F32), high, bias - high]
    base = [jnp.concatenate([weight[core]] + tail, 0) for core in range(2)]
    sub = iota((8, 128), 0)
    mine = (sub == 4) | (sub == 5)
    for m in range(128):
        rows = rows_ref[m * 8 : m * 8 + 8, :]
        out_ref[m] = jnp.where(mine, rows, base[(m // 8) % 2]).astype(BF16)


def weight_rows(ref, out_ref, side):
    upper_rows = iota((8, 128), 0) >= 4
    for p in range(side * 32, side * 32 + 32):
        even, odd = ref[p * 2].astype(F32), ref[p * 2 + 1].astype(F32)
        out_ref[p * 8 : p * 8 + 8, :] = jnp.where(upper_rows, pltpu.roll(odd, 4, 0), even)


def operand_kernel(
    in_ref, update_ref, pair_ref, right_ref, left_ref, bias_ref, rows_ref, plain_ref
):
    for j in range(32):
        at = ((j % 4) * 8 + j // 4) * 16
        plain_ref[pl.ds(j, 16, stride=32), :] = update_ref[at : at + 16, :]
    pair_ref[...] = plain_ref[...].astype(BF16)
    lower = iota((16, 128), 1) < 64
    total = jnp.zeros((8, 128), F32)
    for m in range(128):
        block = in_ref[m].astype(F32)
        rows_ref[m * 8 : m * 8 + 8, :] = block
        total = total + block
    bias_ref[...] = total[6:7] + total[7:8]

    def tiles(row):
        pairs = [
            fold(
                rows_ref[pl.ds(k * 16 + row, 16, stride=64), :],
                rows_ref[pl.ds(k * 16 + 8 + row, 16, stride=64), :],
                lower,
            )
            for k in range(4)
        ]
        return [p[0] for p in pairs], [p[1] for p in pairs]

    for row, out_ref in ((4, right_ref), (5, left_ref)):
        near, far = tiles(row)
        for k, tile in enumerate(near + far):
            for e in range(4):
                out_ref[pl.ds(k * 4 + e, 16, stride=32), :] = tile[:, e * 32 : e * 32 + 32]


def weight_kernel(own_ref, other_ref, out_hbm, rows_ref, sems):
    core = core_index()
    copies = []
    for n, (ref, half) in enumerate(((own_ref, core), (other_ref, 1 - core))):
        for side in range(2):
            weight_rows(ref, rows_ref.at[n], side)
            at = pl.ds(pl.multiple_of(half * 512 + side * 256, 256), 256)
            part = rows_ref.at[n, side * 256 : side * 256 + 256]
            copies.append(pltpu.make_async_copy(part, out_hbm.at[at], sems.at[n * 2 + side]))
            copies[-1].start()
    for copy in copies:
        copy.wait()


def call(kernel, outs, scratch, *args, space=pltpu.VMEM, mib=40, out_space=pltpu.VMEM):
    return pl.pallas_call(
        kernel,
        out_shape=outs,
        in_specs=[pl.BlockSpec(memory_space=space)] * len(args),
        out_specs=tuple([pl.BlockSpec(memory_space=out_space)] * len(outs)),
        scratch_shapes=scratch,
        compiler_params=pltpu.CompilerParams(vmem_limit_bytes=mib * 1024 * 1024),
    )(*args)


def shape(dims, dtype):
    return jax.ShapeDtypeStruct(dims, dtype)


def per_device(left, right, mask, weight, bias, cotangent):
    everyone = [(a, core, b) for a in range(8) for core in range(2) for b in range(8)]

    def place(a, core, b):
        return (a * 2 + core) * 8 + b

    swap = [(place(a, core, b), place(a, 1 - core, b)) for a, core, b in everyone]
    turn = [(place(a, core, b), place(b, core, (a + 4) % 8)) for a, core, b in everyone]
    groups = [[place(a, 0, b) for b in range(8)] for a in range(8)]
    groups += [[place(a, 1, b) for a in range(8)] for b in range(8)]

    def exchange(block, groups=None):
        return lax.all_to_all(block, DEVICES, 0, 0, axis_index_groups=groups, tiled=True)

    def prepared(block):
        (block,) = call(
            prep_kernel,
            (shape((16, 1152), BF16),),
            [
                pltpu.VMEM((512, 32), BF16),
                pltpu.VMEM((16, 32), jnp.int32),
                pltpu.VMEM((512, 32), F32),
                pltpu.SemaphoreType.DMA((5,)),
            ],
            block.reshape(512, 32),
            mask,
            space=pltpu.HBM,
            mib=60,
        )
        return block

    left_block, right_block = prepared(left), prepared(right)
    bias = jnp.broadcast_to(bias, (8, 128))
    left_block, bias = lax.optimization_barrier((lax.ppermute(left_block, DEVICES, turn), bias))
    other_right = lax.ppermute(right_block, DEVICES, swap)
    other_left = lax.ppermute(left_block, DEVICES, swap)
    first = core_index() == 0
    near = jnp.where(first, left_block, other_right)
    far = jnp.where(first, other_left, right_block)
    block = jnp.concatenate([near[:, :1024], far[:, :1024], near[:, 1024:] + far[:, 1024:]], 1)
    own = exchange(jnp.broadcast_to(block, (8, 16, 2176)), groups).reshape(128, 2176)
    own, cotangent = lax.optimization_barrier((own, cotangent))
    other = lax.ppermute(own, DEVICES, swap)
    cot_rows, bias_part = call(
        cotangent_kernel,
        (shape((512, 128), F32), shape((1, 128), F32)),
        [pltpu.VMEM((512, 128), F32)],
        cotangent.reshape(512, 128),
    )
    lanes, order = lane_order(), row_order()

    weight = weight.reshape(1024, 128)
    send, outer, outer_grad, left_all, right_all, mask_i, mask_jd, scaled, inverse = call(
        outer_kernel,
        (
            shape((256, 768), BF16),
            shape((512, 1024), BF16),
            shape((512, 1024), BF16),
            shape((256, 512), BF16),
            shape((256, 1024), BF16),
            shape((256, 512), BF16),
            shape((256, 1024), BF16),
            shape((512, 128), BF16),
            shape((512, 128), F32),
        ),
        [pltpu.VMEM((512, 1024), F32), pltpu.VMEM((512, 1024), F32)],
        own,
        other,
        lanes,
        mask_spread(),
        weight,
        cot_rows,
    )
    got = lax.ppermute(send, DEVICES, swap)
    update, right_sum, weight_sum, left_sum = call(
        sums_kernel,
        (shape((512, 128), F32), shape((256, 512), F32), shape((512, 128), F32), shape((256, 512), F32)),
        [],
        outer,
        outer_grad,
        left_all,
        right_all,
        mask_i,
        mask_jd,
        scaled,
        inverse,
        lanes,
        order,
        weight,
        bias,
    )
    (parts,) = call(
        pack_kernel,
        (shape((128, 4, 640), BF16),),
        [pltpu.VMEM((256, 512), F32)],
        got,
        right_sum,
        weight_sum,
        left_sum,
        order,
    )
    parts = exchange(parts)
    (sums,) = call(
        reduce_kernel, (shape((128, 8, 128), BF16),), [pltpu.VMEM((1024, 128), F32)], parts, bias_part
    )
    sums = exchange(sums)
    other_sums = lax.ppermute(sums, DEVICES, swap)
    pair_update, right_grad, left_grad, bias_grad = call(
        operand_kernel,
        (shape((512, 128), BF16), shape((512, 32), F32), shape((512, 32), F32), shape((1, 128), F32)),
        [pltpu.VMEM((1024, 128), F32), pltpu.VMEM((512, 128), F32)],
        sums,
        update,
    )
    (weight_grad,) = call(
        weight_kernel,
        (shape((1024, 128), F32),),
        [pltpu.VMEM((2, 512, 128), F32), pltpu.SemaphoreType.DMA((4,))],
        sums,
        other_sums,
        out_space=pltpu.HBM,
    )
    return (
        pair_update.reshape(16, 32, 128),
        left_grad.reshape(16, 32, 32),
        right_grad.reshape(16, 32, 32),
        weight_grad.reshape(32, 32, 128),
        bias_grad.reshape(128),
    )


def solution(mesh):
    return jax.shard_map(
        per_device,
        mesh=mesh,
        in_specs=(
            P("seq", "res", None),
            P("seq", "res", None),
            P("seq", "res"),
            P(),
            P(),
            P("seq", "res", None),
        ),
        out_specs=(P("seq", "res", None), P("seq", "res", None), P("seq", "res", None), P(), P()),
        check_vma=False,
    )
```
